32 devices in a mesh: expert: 8 (over z, core), context: 2 (over x), dp: 2 (over y).
Axes of the slice: x: 2, y: 2, z: 4, core: 2. Of those that a mesh axis runs over, the one named last changes fastest.
Arguments:
- tokens_in: bfloat16 [8, 512, 2048], P('expert', ('context', 'dp')), may hold values from -6 to 6
- doc_ids: int32 [8, 512], P('expert'), may hold values from 0 to 2, as said below
- routes: int32 [8, 512, 6], P('expert', ('context', 'dp')), may hold values from 0 to 15, all different within a row; in each aligned block of 128 rows (0 to 127, 128 to 255, ..., all dimensions but the last counted through in order) at most 64 rows name the same one
- gain_attn: bfloat16 [2048], P(('expert', 'context', 'dp')), may hold values from 0.5 to 1.5
- w_query: bfloat16 [2048, 2048], P(('expert', 'context', 'dp')), may hold values from -0.125 to 0.125
- w_key: bfloat16 [2048, 2048], P(('expert', 'context', 'dp')), may hold values from -0.125 to 0.125
- w_value: bfloat16 [2048, 2048], P(('expert', 'context', 'dp')), may hold values from -0.125 to 0.125
- w_out: bfloat16 [2048, 2048], P(('expert', 'context', 'dp')), may hold values from -0.5 to 0.5
- gain_moe: bfloat16 [2048], P(('expert', 'context', 'dp')), may hold values from 0.5 to 1.5
- w_router: bfloat16 [2048, 16], P(('expert', 'context', 'dp')), may hold values from -0.0625 to 0.0625
- shared_gate: bfloat16 [2048, 2816], P(('expert', 'context', 'dp')), may hold values from -0.125 to 0.125
- shared_up: bfloat16 [2048, 2816], P(('expert', 'context', 'dp')), may hold values from -0.125 to 0.125
- shared_down: bfloat16 [2816, 2048], P(('expert', 'context', 'dp')), may hold values from -0.109375 to 0.109375
- expert_gate: bfloat16 [16, 2048, 1408], P('expert', ('context', 'dp')), may hold values from -0.125 to 0.125
- expert_up: bfloat16 [16, 2048, 1408], P('expert', ('context', 'dp')), may hold values from -0.125 to 0.125
- expert_down: bfloat16 [16, 1408, 2048], P('expert', ('context', 'dp')), may hold values from -0.875 to 0.875
- cotangent: bfloat16 [8, 512, 2048], P('expert', ('context', 'dp')), may hold values from -6 to 6
Outputs:
- layer_out: float32 [8, 512, 2048], P('expert', ('context', 'dp'))
- grad_tokens: float32 [8, 512, 2048], P('expert', ('context', 'dp'))
- grad_gain_attn: float32 [2048], P(('expert', 'context', 'dp'))
- grad_query: float32 [2048, 2048], P(('expert', 'context', 'dp'))
- grad_key: float32 [2048, 2048], P(('expert', 'context', 'dp'))
- grad_value: float32 [2048, 2048], P(('expert', 'context', 'dp'))
- grad_out: float32 [2048, 2048], P(('expert', 'context', 'dp'))
- grad_gain_moe: float32 [2048], P(('expert', 'context', 'dp'))
- grad_router: float32 [2048, 16], P(('expert', 'context', 'dp'))
- grad_shared_gate: float32 [2048, 2816], P(('expert', 'context', 'dp'))
- grad_shared_up: float32 [2048, 2816], P(('expert', 'context', 'dp'))
- grad_shared_down: float32 [2816, 2048], P(('expert', 'context', 'dp'))
- grad_expert_gate: float32 [16, 2048, 1408], P('expert', ('context', 'dp'))
- grad_expert_up: float32 [16, 2048, 1408], P('expert', ('context', 'dp'))
- grad_expert_down: float32 [16, 1408, 2048], P('expert', ('context', 'dp'))
The draws below stay inside these ranges and needn't reach their ends.
Inputs may be any that keep to these rules, and one draw needn't show every extreme that they name: `doc_ids`: Non-decreasing along each sequence, starting at 0 and rising by at most one from one position to the next. `routes`: A token names 6 different experts. Among the 128 tokens of one device no expert is named more than 64 times, a bound that some block reaches.
All inputs are finite; a program needn't handle non-finite values.
Results may differ from the reference program's by a relative error of at most 0.018.
Values may be sent and summed in bfloat16 or wider, within the bound.
No kernel may reach another device: no remote copies, remote signals or barrier semaphores. Data moves between devices by JAX's collectives and lax.ppermute only.
A program may use at most 448 MiB of HBM per device.

```python
import math
import jax
import jax.numpy as jnp
import numpy as np
from jax import lax

MODEL_DIM = 2048
HEADS = 16
HD = 128
H = 1408
SH = 2816
TOP = 6
GROUP = 128
EXPERTS = 16
SEQUENCE_TOKENS = 512
SEQS = 8
CAP = 64


def draw_doc_ids(key, part):
    key = jax.random.fold_in(key, 11)
    first_key, second_key = jax.random.split(key)
    first_end = jax.random.randint(first_key, (SEQS, 1), 1, GROUP)
    second_end = jax.random.randint(second_key, (SEQS, 1), SEQUENCE_TOKENS - GROUP + 1, SEQUENCE_TOKENS)
    positions = jnp.arange(SEQUENCE_TOKENS, dtype=jnp.int32)[None, :]
    return (positions >= first_end).astype(jnp.int32) + (positions >= second_end).astype(jnp.int32)


def shard_levels(key, extent, cuts, low, top_value):
    def one(axis_at, parts):
        steps = jax.random.uniform(jax.random.fold_in(jax.random.fold_in(key, 6), axis_at), (parts,), jnp.float32, low / len(cuts), top_value / len(cuts))
        return jnp.repeat(jnp.exp(steps), extent[axis_at] // parts).reshape((-1,) + (1,) * (len(extent) - axis_at - 1))

    level = one(*cuts[0])
    for cut in cuts[1:]:
        level = level * one(*cut)
    return level


def deal_out(key, own, number, rows, number_of, top, limit, lean):
    order = jax.random.permutation(key, number_of)
    packed, common = load_shares(number_of, rows * top, limit, lean, True), load_shares(number_of, rows * top, limit, lean, False)
    places = jnp.arange(number_of)

    def named(sizes, rotation):
        used = int((sizes > 0).sum())
        fixed = max(1, used // 4)
        passed = fixed + (places - fixed + rotation * (used - fixed)) % max(1, number_of - fixed)
        return jnp.zeros((number_of,), jnp.int32).at[order[jnp.where(places < fixed, places, passed)]].set(jnp.asarray(sizes, jnp.int32))

    sizes = jnp.where(number % 4 == 0, named(packed, number // 4), named(common, number - number // 4 - 1))
    mixed = jax.random.permutation(jax.random.fold_in(own, 3), number_of)
    source_of, taker = mixed[0:number_of // 2 * 2:2], mixed[1:number_of // 2 * 2:2]
    margin = jnp.minimum(sizes[source_of] - 1, limit - sizes[taker]) // 2
    margin = jnp.where((source_of == order[0]) | (taker == order[0]) | (sizes[taker] == 0), 0, jnp.maximum(margin, 0))
    passed = jax.random.randint(jax.random.fold_in(own, 4), (number_of // 2,), 0, 1 << 20) % (margin + 1)
    sizes = sizes.at[source_of].add(-passed).at[taker].add(passed)
    members = jnp.searchsorted(jnp.cumsum(sizes), jnp.arange(rows * top), side="right").astype(jnp.int32)
    grid = members.reshape(top, rows).T
    grid = grid[jax.random.permutation(jax.random.fold_in(own, 1), rows)]
    rotation = jax.random.randint(jax.random.fold_in(own, 2), (rows, 1), 0, top)
    return jnp.take_along_axis(grid, (jnp.arange(top)[None, :] + rotation) % top, axis=1)


def load_shares(count, total, reach, lean, full):
    weights = [(1 << 20) // math.isqrt(rank ** lean) + 1 for rank in range(1, count + 1)]
    largest = reach if full else min(reach, max(-(-total // count), total * weights[0] // sum(weights)))
    least = 1 if total - largest >= count - 1 else 0
    counts, surplus = [largest] + [least] * (count - 1), total - largest - least * (count - 1)
    while surplus > 0:
        candidates = [i for i in range(1, count) if counts[i] < largest] or [i for i in range(1, count) if counts[i] < reach]
        whole, remaining = sum([weights[i] for i in candidates]), surplus
        for i in candidates:
            extra = min(reach - counts[i], max(1, remaining * weights[i] // whole), surplus)
            counts[i] = counts[i] + extra
            surplus = surplus - extra
    return np.array(counts)


def scatter_about(own_key, shape, width, reach, shards=(), kind=jnp.bfloat16):
    drawn = jax.random.normal(own_key, shape, jnp.float32) * width
    if len(shards) > 0:
        drawn = shard_levels(own_key, shape, shards, -0.22, 0.18) * drawn
    return jnp.clip(drawn, min=-reach, max=reach).astype(kind)


def setup_inputs(seed: int = 0) -> dict:
    key_of = jax.random.split(jax.random.key(seed), 18)
    tokens_in = scatter_about(key_of[0], (SEQS, SEQUENCE_TOKENS, MODEL_DIM), 1.0, 6.0, ((0, 8), (1, 4)))
    doc_ids = draw_doc_ids(jax.random.fold_in(key_of[17], 71), 0)
    routes_keys = jax.random.split(jax.random.fold_in(key_of[2], 1), SEQS * SEQUENCE_TOKENS // GROUP)
    routes_turns = jax.random.permutation(jax.random.fold_in(key_of[2], 3), SEQS * SEQUENCE_TOKENS // GROUP)
    routes = jax.vmap(lambda own, number: deal_out(jax.random.fold_in(key_of[2], 2), own, number, GROUP, EXPERTS, TOP, CAP, 1))(routes_keys, routes_turns).reshape((SEQS, SEQUENCE_TOKENS, TOP))
    gain_attn = jnp.clip(1.0 + 0.1 * jax.random.normal(key_of[3], (MODEL_DIM,), jnp.float32), 0.5, 1.5).astype(jnp.bfloat16)
    w_query = scatter_about(key_of[4], (MODEL_DIM, MODEL_DIM), MODEL_DIM ** -0.5, 0.125, ((0, 32),))
    w_key = scatter_about(key_of[5], (MODEL_DIM, MODEL_DIM), MODEL_DIM ** -0.5, 0.125, ((0, 32),))
    w_value = scatter_about(key_of[6], (MODEL_DIM, MODEL_DIM), MODEL_DIM ** -0.5, 0.125, ((0, 32),))
    w_out = scatter_about(key_of[7], (MODEL_DIM, MODEL_DIM), (MODEL_DIM // 16) ** -0.5, 0.5, ((0, 32),))
    gain_moe = jnp.clip(1.0 + 0.1 * jax.random.normal(key_of[8], (MODEL_DIM,), jnp.float32), 0.5, 1.5).astype(jnp.bfloat16)
    w_router = scatter_about(key_of[9], (MODEL_DIM, EXPERTS), (4 * MODEL_DIM) ** -0.5, 0.0625, ((0, 32),))
    shared_gate = scatter_about(key_of[10], (MODEL_DIM, SH), MODEL_DIM ** -0.5, 0.125, ((0, 32),))
    shared_up = scatter_about(key_of[11], (MODEL_DIM, SH), MODEL_DIM ** -0.5, 0.125, ((0, 32),))
    shared_down = scatter_about(key_of[12], (SH, MODEL_DIM), SH ** -0.5, 0.109375, ((0, 32),))
    expert_gate = scatter_about(key_of[13], (EXPERTS, MODEL_DIM, H), MODEL_DIM ** -0.5, 0.125, ((0, 8), (1, 4)))
    expert_up = scatter_about(key_of[14], (EXPERTS, MODEL_DIM, H), MODEL_DIM ** -0.5, 0.125, ((0, 8), (1, 4)))
    expert_down = scatter_about(key_of[15], (EXPERTS, H, MODEL_DIM), (max(1, H * TOP * TOP // (4 * EXPERTS * EXPERTS))) ** -0.5, 0.875, ((0, 8), (1, 4)))
    cotangent = scatter_about(key_of[16], (SEQS, SEQUENCE_TOKENS, MODEL_DIM), 1.0, 6.0, ((0, 8), (1, 4)))
    return dict(tokens_in=tokens_in, doc_ids=doc_ids, routes=routes, gain_attn=gain_attn, w_query=w_query, w_key=w_key, w_value=w_value, w_out=w_out, gain_moe=gain_moe, w_router=w_router, shared_gate=shared_gate, shared_up=shared_up, shared_down=shared_down, expert_gate=expert_gate, expert_up=expert_up, expert_down=expert_down, cotangent=cotangent)


EPS = 1e-06
MASKED = -1e+30
HIGH = lax.Precision.HIGHEST

@jax.custom_vjp
def low(v):
    return lax.optimization_barrier(v.astype(jnp.bfloat16)).astype(jnp.float32)

@jax.custom_vjp
def low_back(v):
    return v

def low_keep(v):
    return (low(v), None)

def low_pass(kept, grad):
    return (grad,)

def back_keep(v):
    return (v, None)

def back_low(kept, grad):
    return (low(grad),)
low.defvjp(low_keep, low_pass)
low_back.defvjp(back_keep, back_low)

def matmul(left, right):
    return jnp.dot(left, right, precision=HIGH, preferred_element_type=jnp.float32)

def rms_scale(values, gain):
    return values * lax.rsqrt(lax.optimization_barrier(jnp.mean(values * values, axis=-1, keepdims=True)) + EPS) * gain

def rope_tables(doc_row, head_size):
    seq_length = doc_row.shape[0]
    positions = jnp.arange(seq_length, dtype=jnp.int32)
    doc_starts = lax.optimization_barrier(jnp.sum((doc_row[None, :] < doc_row[:, None]).astype(jnp.int32), axis=1))
    offsets = (positions - doc_starts).astype(jnp.float32)
    half_size = head_size // 2
    frequency = jnp.exp(jnp.arange(half_size, dtype=jnp.float32) * (-math.log(10000.0) / half_size))
    angles = offsets[:, None] * frequency[None, :]
    return (jnp.cos(angles), jnp.sin(angles))

def rotate(values, cosine, sine):
    half_size = values.shape[-1] // 2
    first_half = values[..., :half_size]
    second_half = values[..., half_size:]
    cos_heads = cosine[:, None, :]
    sin_heads = sine[:, None, :]
    return jnp.concatenate([first_half * cos_heads - second_half * sin_heads, second_half * cos_heads + first_half * sin_heads], axis=-1)

def layer(inputs, layer_parameters, doc_row, route_row):
    first_norm_gain, query_matrix, key_matrix, value_matrix, output_matrix, second_norm_gain, router_matrix, shared_gate_matrix, shared_up_matrix, shared_down_matrix, every_expert_gate, every_expert_up, every_expert_down = layer_parameters
    cosine, sine = rope_tables(doc_row, HD)
    normed_one = low(rms_scale(inputs, first_norm_gain))
    query_pre = low_back(matmul(normed_one, query_matrix)).reshape(SEQUENCE_TOKENS, HEADS, HD)
    key_pre = low_back(matmul(normed_one, key_matrix)).reshape(SEQUENCE_TOKENS, HEADS, HD)
    value_heads = low(low_back(matmul(normed_one, value_matrix))).reshape(SEQUENCE_TOKENS, HEADS, HD)
    query_rot = low(rotate(query_pre, cosine, sine))
    key_rot = low(rotate(key_pre, cosine, sine))
    scores = low_back(jnp.einsum('qhd,khd->hqk', query_rot, key_rot, precision=HIGH) * HD ** (-0.5))
    positions = jnp.arange(SEQUENCE_TOKENS, dtype=jnp.int32)
    allowed = (positions[:, None] >= positions[None, :]) & (doc_row[:, None] == doc_row[None, :])
    scores = jnp.where(allowed[None], scores, MASKED)
    exponent = jnp.exp(scores - lax.optimization_barrier(jnp.max(scores, axis=2, keepdims=True)))
    coefficients_reduced = low(exponent / lax.optimization_barrier(jnp.sum(exponent, axis=2, keepdims=True)))
    mixed = low(low_back(jnp.einsum('hqk,khd->qhd', coefficients_reduced, value_heads, precision=HIGH))).reshape(SEQUENCE_TOKENS, MODEL_DIM)
    after_attn = inputs + low_back(matmul(mixed, output_matrix))
    normed_two = low(rms_scale(after_attn, second_norm_gain))
    logits = low_back(matmul(normed_two, router_matrix))
    router_exp = jnp.exp(logits - lax.optimization_barrier(jnp.max(logits, axis=1, keepdims=True)))
    router_probs = router_exp / lax.optimization_barrier(jnp.sum(router_exp, axis=1, keepdims=True))
    chosen = lax.optimization_barrier(jnp.sum((route_row[:, :, None] == jnp.arange(EXPERTS, dtype=jnp.int32)[None, None, :]).astype(jnp.float32), axis=1))
    gate_matrix = router_probs * chosen
    shared_a = low_back(matmul(normed_two, shared_gate_matrix))
    shared_b = low_back(matmul(normed_two, shared_up_matrix))
    shared_out = low_back(matmul(low(jax.nn.silu(shared_a) * shared_b), shared_down_matrix))

    def single_expert(running, pieces):
        gate_weight, up_weight, down_weight, gate_column = pieces
        given = low_back(normed_two)
        pre_gate = low_back(matmul(given, gate_weight))
        preactivation_up = low_back(matmul(given, up_weight))
        made = low(low_back(matmul(low(jax.nn.silu(pre_gate) * preactivation_up), down_weight)))
        return (running + gate_column[:, None] * made, None)
    dispatched_pieces, ignored_value = lax.scan(jax.checkpoint(single_expert), jnp.zeros((SEQUENCE_TOKENS, MODEL_DIM), jnp.float32), (every_expert_gate, every_expert_up, every_expert_down, gate_matrix.T))
    return after_attn + dispatched_pieces + shared_out

def reference(tokens_in, doc_ids, routes, gain_attn, w_query, w_key, w_value, w_out, gain_moe, w_router, shared_gate, shared_up, shared_down, expert_gate, expert_up, expert_down, cotangent):
    layer_parameters = tuple((weight.astype(jnp.float32) for weight in (gain_attn, w_query, w_key, w_value, w_out, gain_moe, w_router, shared_gate, shared_up, shared_down, expert_gate, expert_up, expert_down)))

    def per_sequence(running, pieces):
        token_row, doc_row, route_row, adjoint_line = pieces

        def forward(inputs, weights):
            return layer(inputs, weights, doc_row, route_row)
        out_row, pull_back = jax.vjp(forward, token_row.astype(jnp.float32), layer_parameters)
        grad_row, grad_params = pull_back(adjoint_line.astype(jnp.float32))
        running = tuple((left + right for left, right in zip(running, grad_params)))
        return (running, (out_row, grad_row))
    zeros_start = tuple((jnp.zeros_like(weight) for weight in layer_parameters))
    totals, outputs = lax.scan(per_sequence, zeros_start, (tokens_in, doc_ids, routes, cotangent))
    return (outputs[0], outputs[1], totals[0], totals[1], totals[2], totals[3], totals[4], totals[5], totals[6], totals[7], totals[8], totals[9], totals[10], totals[11], totals[12])
```

```python
import math

import jax
import jax.numpy as jnp
from jax import lax
from jax.sharding import Mesh
from jax.sharding import PartitionSpec as P

HD = 128
TOP = 6
EPS = 1e-06
MASKED = -1e30
Z, K, C, D = "z", "core", "context", "dp"
F32 = jnp.float32
LOW = jnp.bfloat16


class Line:
    def __init__(self, mesh, *names):
        self.names = names
        self.size = math.prod(mesh.shape[name] for name in names)

    def at(self):
        return lax.axis_index(self.names)

    def swap(self, value, delta):
        return lax.ppermute(value, self.names, [(i, i ^ delta) for i in range(self.size)])

    def share(self, value):
        return [value] + [self.swap(value, delta) for delta in range(1, self.size)]

    def give(self, pieces):
        return [pieces[0]] + [self.swap(pieces[delta], delta) for delta in range(1, self.size)]

    def give_from(self, stack, dim=0):
        here = self.at()
        return self.give([pick(stack, here ^ delta, dim) for delta in range(self.size)])


def pick(stack, index, dim=0):
    return lax.dynamic_index_in_dim(stack, index, dim, keepdims=False)


def settle(pieces, index, dim=0):
    shape = list(pieces[0].shape)
    shape.insert(dim, len(pieces))
    out = jnp.zeros(shape, pieces[0].dtype)
    for delta, piece in enumerate(pieces):
        out = lax.dynamic_update_index_in_dim(out, piece, index ^ delta, dim)
    return out


def dot(left, right):
    return jnp.dot(left, right, preferred_element_type=F32)


def total(pieces):
    out = pieces[0].astype(F32)
    for piece in pieces[1:]:
        out = out + piece.astype(F32)
    return out


def turn(values, cosine, sine, sign):
    half = HD // 2
    first, second = values[..., :half], values[..., half:]
    return jnp.concatenate(
        [first * cosine - sign * second * sine, second * cosine + sign * first * sine], axis=-1
    )


def norm_back(grad_normed, normed, scale, gain):
    scaled = grad_normed * gain
    return scale * (scaled - normed * jnp.mean(scaled * normed, axis=1, keepdims=True))


def swish_slope(values, sigma):
    return sigma * (1.0 + values * (1.0 - sigma))


def make_body(mesh):
    line_z, line_k, line_t = Line(mesh, Z), Line(mesh, K), Line(mesh, C, D)
    line_e = Line(mesh, Z, K)
    columns, cores, blocks, owners = line_z.size, line_k.size, line_t.size, line_e.size

    def body(
        tokens_in,
        doc_ids,
        routes,
        gain_attn,
        w_query,
        w_key,
        w_value,
        w_out,
        gain_moe,
        w_router,
        shared_gate,
        shared_up,
        shared_down,
        expert_gate,
        expert_up,
        expert_down,
        cotangent,
    ):
        col, core, blk = line_z.at(), line_k.at(), line_t.at()
        x_low, dy_low = tokens_in[0], cotangent[0]
        rows, width = x_low.shape
        length = doc_ids.shape[1]
        part = w_query.shape[0]
        span = width // blocks
        heads = span // HD
        experts = w_router.shape[1]
        group = experts // columns
        line_s = line_t if blocks == group else Line(mesh, C)
        rest = () if blocks == group else (D,)
        spot = line_s.at()

        small = jnp.concatenate([w_router.T, gain_attn[None], gain_moe[None]], axis=0)
        small = settle(line_t.share(small), blk)
        small = settle(line_e.share(small), line_e.at())
        small = small.transpose(2, 0, 1, 3).reshape(experts + 2, width)
        router_t = small[:experts]
        gain_first = small[experts].astype(F32)[None]
        gain_second = small[experts + 1].astype(F32)[None]

        mixed_in = jnp.concatenate(
            [w.reshape(part, blocks, span) for w in (w_query, w_key, w_value)], axis=2
        ).transpose(1, 0, 2)
        qkv = settle(line_t.give_from(mixed_in), blk).reshape(blocks * part, 3 * span)
        qkv = lax.all_gather(qkv, (Z, K), axis=0, tiled=True)
        move = [(i, (i % owners) * blocks + i // owners) for i in range(owners * blocks)]
        out_mat = lax.ppermute(w_out, (Z, K, C, D), move)
        out_mat = lax.all_gather(out_mat, (Z, K), axis=0, tiled=True)

        x_all = jnp.concatenate(line_t.share(x_low), axis=0).astype(F32)
        inputs = x_low.astype(F32)

        def fetch(weight):
            local, count, wide = weight.shape
            halves = weight.reshape(local, cores, count // cores, wide)
            other = line_k.swap(pick(halves, 1 - core, 1), 1)
            both = settle([pick(halves, core, 1), other], core)
            got = line_s.give_from(both.reshape(group, count // cores, wide))
            pieces = []
            for piece in got:
                pieces += [piece, line_k.swap(piece, 1)]
            whole = settle(pieces, spot * cores + core).reshape(line_s.size, count, wide)
            if rest:
                whole = lax.all_gather(whole, rest, axis=1, tiled=True)
            return whole.reshape(-1, wide)

        def fetch_shared(piece, dim):
            got = line_t.share(piece)
            pieces = got + [line_k.swap(one, 1) for one in got]
            return settle(pieces, core * blocks + blk, dim)

        hidden = shared_gate.shape[1] // columns
        both_in = jnp.concatenate(
            [w.reshape(part, columns, hidden) for w in (shared_gate, shared_up)], axis=2
        ).transpose(1, 0, 2)
        both_in = settle(line_z.give_from(both_in), col)

        dy_col = lax.all_gather(dy_low, Z, axis=0, tiled=True)
        routes_col = settle(line_z.share(routes[0]), col)

        mat_down = fetch(expert_down)
        mat_sdown = fetch_shared(shared_down, 0).reshape(hidden, width)
        mat_gate = fetch(expert_gate)
        mat_up = fetch(expert_up)
        mat_sin = fetch_shared(both_in, 1).reshape(width, 2 * hidden)

        doc_row = doc_ids[0]
        order = blk ^ jnp.arange(blocks, dtype=jnp.int32)
        doc_starts = jnp.sum((doc_row[None, :] < doc_row[:, None]).astype(jnp.int32), axis=1)
        offsets = jnp.arange(length, dtype=jnp.int32) - doc_starts

        def reorder(row):
            grid = row.reshape(blocks, rows)
            return jnp.concatenate([pick(grid, order[i]) for i in range(blocks)])

        doc_here, off_here = reorder(doc_row), reorder(offsets)
        place = reorder(jnp.arange(length, dtype=jnp.int32))
        frequency = jnp.exp(
            jnp.arange(HD // 2, dtype=F32) * (-math.log(10000.0) / (HD // 2))
        )
        angles = off_here.astype(F32)[:, None] * frequency[None, :]
        cosine, sine = jnp.cos(angles)[:, None, :], jnp.sin(angles)[:, None, :]
        allowed = (place[:, None] >= place[None, :]) & (doc_here[:, None] == doc_here[None, :])

        first_scale = lax.rsqrt(jnp.mean(x_all * x_all, axis=1, keepdims=True) + EPS)
        first_normed = x_all * first_scale
        normed_low = (first_normed * gain_first).astype(LOW)
        made = dot(normed_low, qkv)

        def per_head(values):
            return values.reshape(length, heads, HD)

        query_low = turn(per_head(made[:, :span]), cosine, sine, 1.0).astype(LOW)
        key_low = turn(per_head(made[:, span : 2 * span]), cosine, sine, 1.0).astype(LOW)
        value_low = per_head(made[:, 2 * span :].astype(LOW))
        score_scale = HD ** (-0.5)
        scores = jnp.einsum("qhd,khd->hqk", query_low, key_low, preferred_element_type=F32)
        scores = jnp.where(allowed[None], scores * score_scale, MASKED)
        exponent = jnp.exp(scores - jnp.max(scores, axis=2, keepdims=True))
        attn_probs = exponent / jnp.sum(exponent, axis=2, keepdims=True)
        probs_low = attn_probs.astype(LOW)
        mixed_low = (
            jnp.einsum("hqk,khd->qhd", probs_low, value_low, preferred_element_type=F32)
            .astype(LOW)
            .reshape(length, span)
        )
        attn_out = dot(mixed_low, out_mat).astype(LOW).reshape(blocks, rows, width)
        after_attn = inputs + total(line_t.give([attn_out[i] for i in range(blocks)]))

        second_scale = lax.rsqrt(jnp.mean(after_attn * after_attn, axis=1, keepdims=True) + EPS)
        second_normed = after_attn * second_scale
        second_low = (second_normed * gain_second).astype(LOW)
        second_col = lax.all_gather(second_low, Z, axis=0, tiled=True)

        def router(values):
            return jax.nn.softmax(dot(values, router_t.T), axis=1)

        router_probs = router(second_low)
        probs_col = router(second_col)

        capacity = min(rows, rows * TOP * 4 // (3 * experts))
        slots = columns * capacity
        wanted = col * group + (spot ^ jnp.arange(group, dtype=jnp.int32))
        hits = jnp.any(routes_col[None] == wanted[:, None, None, None], axis=3)
        ranks = jnp.cumsum(hits.astype(jnp.int32), axis=2) - 1
        ranks = jnp.where(hits, ranks, -1)
        chosen = ranks[:, :, None, :] == jnp.arange(capacity, dtype=jnp.int32)[:, None]
        same = jnp.eye(columns, dtype=jnp.bool_)[None, :, None, :, None]
        spread = (
            (chosen[:, :, :, None, :] & same).reshape(group * slots, columns * rows).astype(LOW)
        )

        def dispatch(values):
            sent = dot(spread, values).astype(LOW).reshape(group, slots, width)
            return jnp.concatenate(line_s.give([sent[i] for i in range(group)]), axis=0)

        def collect(values):
            parts = values.reshape(group, slots, width)
            back = line_s.give([parts[i] for i in range(group)])
            return dot(spread.T, jnp.concatenate(back, axis=0))

        dy_slots = dispatch(dy_col)
        du_raw = dot(dy_slots, mat_down.T)
        gate_col = jnp.sum(
            jnp.where(
                jnp.arange(experts, dtype=jnp.int32) == wanted[:, None, None], probs_col[None], 0.0
            ),
            axis=2,
        ).reshape(group, columns, 1, rows)
        gate_sent = jnp.sum(jnp.where(chosen, gate_col, 0.0), axis=3).reshape(group, 1, slots)
        gate = jnp.concatenate(line_s.give([gate_sent[i] for i in range(group)]), axis=1)
        gate = gate.reshape(group * slots, 1)

        second_slots = dispatch(second_col)
        pre_gate = dot(second_slots, mat_gate)
        pre_up = dot(second_slots, mat_up)
        sigma = jax.nn.sigmoid(pre_gate)
        hidden_low = (pre_gate * sigma * pre_up).astype(LOW)
        dgate = jnp.sum(hidden_low.astype(F32) * du_raw, axis=1)
        du = du_raw * gate
        grad_a = (du * pre_up * swish_slope(pre_gate, sigma)).astype(LOW)
        grad_b = (du * pre_gate * sigma).astype(LOW)
        grad_slots = (dot(grad_a, mat_gate.T) + dot(grad_b, mat_up.T)).astype(LOW)

        shared_pre = dot(second_col, mat_sin)
        shared_a, shared_b = shared_pre[:, :hidden], shared_pre[:, hidden:]
        shared_sigma = jax.nn.sigmoid(shared_a)
        shared_low = (shared_a * shared_sigma * shared_b).astype(LOW)
        dsu = dot(dy_col, mat_sdown.T)
        dsa = (dsu * shared_b * swish_slope(shared_a, shared_sigma)).astype(LOW)
        dsb = (dsu * shared_a * shared_sigma).astype(LOW)
        dsab = jnp.concatenate([dsa, dsb], axis=1)

        grad_second = (dot(dsab, mat_sin.T) + collect(grad_slots)).astype(LOW)
        grad_second = lax.psum_scatter(grad_second, Z, scatter_dimension=0, tiled=True)

        dgate_parts = dgate.reshape(group, 1, slots)
        dgate_back = line_s.give([dgate_parts[i] for i in range(group)])
        dgate_back = jnp.stack(dgate_back).reshape(group, columns, capacity, 1)
        dgate_col = jnp.sum(jnp.where(chosen, dgate_back, 0.0), axis=2)
        dgate_col = settle([dgate_col[i] for i in range(group)], spot)
        dprobs = settle(line_z.give_from(dgate_col.transpose(1, 0, 2)), col)
        dprobs = dprobs.reshape(experts, rows).T
        dlogits = (
            router_probs * (dprobs - jnp.sum(dprobs * router_probs, axis=1, keepdims=True))
        ).astype(LOW)
        grad_router_t = dot(dlogits.T, second_low)
        grad_second = grad_second.astype(F32) + dot(dlogits, router_t)

        grad_gain_second = jnp.sum(grad_second * second_normed, axis=0, keepdims=True)
        dy = dy_low.astype(F32)
        grad_after = dy + norm_back(grad_second, second_normed, second_scale, gain_second)
        grad_after_low = jnp.concatenate(line_t.share(grad_after.astype(LOW)), axis=0)

        grad_mixed = per_head(dot(grad_after_low, out_mat.T).astype(LOW))
        grad_outmat = dot(mixed_low.T, grad_after_low).astype(LOW)
        grad_probs = jnp.einsum("qhd,khd->hqk", grad_mixed, value_low, preferred_element_type=F32)
        grad_value = jnp.einsum("hqk,qhd->khd", probs_low, grad_mixed, preferred_element_type=F32)
        grad_scores = (
            attn_probs * (grad_probs - jnp.sum(grad_probs * attn_probs, axis=2, keepdims=True))
        ).astype(LOW)
        grad_query = jnp.einsum("hqk,khd->qhd", grad_scores, key_low, preferred_element_type=F32)
        grad_key = jnp.einsum("hqk,qhd->khd", grad_scores, query_low, preferred_element_type=F32)
        grad_query = turn(grad_query * score_scale, cosine, sine, -1.0)
        grad_key = turn(grad_key * score_scale, cosine, sine, -1.0)
        grad_made = jnp.concatenate(
            [g.astype(LOW).reshape(length, span) for g in (grad_query, grad_key, grad_value)], axis=1
        )
        grad_qkv = dot(normed_low.T, grad_made).astype(LOW)
        grad_first = dot(grad_made, qkv.T).astype(LOW).reshape(blocks, rows, width)
        grad_first = total(line_t.give([grad_first[i] for i in range(blocks)]))
        local_normed = first_normed[:rows]
        grad_gain_first = jnp.sum(grad_first * local_normed, axis=0, keepdims=True)
        grad_inputs = grad_after + norm_back(
            grad_first, local_normed, first_scale[:rows], gain_first
        )

        routed = (dot(hidden_low, mat_down) * gate).astype(LOW)
        layer_out = (dot(shared_low, mat_sdown) + collect(routed)).astype(LOW)
        layer_out = lax.psum_scatter(layer_out, Z, scatter_dimension=0, tiled=True)
        layer_out = after_attn + layer_out.astype(F32)

        def deliver(grad, local, count):
            wide = grad.shape[1]
            grad = grad.astype(LOW).reshape(line_s.size, -1, wide)
            if rest:
                grad = lax.psum_scatter(grad, rest, scatter_dimension=1, tiled=True)
            grad = grad.reshape(line_s.size, cores, count // cores, wide)
            mine = total([pick(grad, core, 1), line_k.swap(pick(grad, 1 - core, 1), 1)])
            got = settle(line_s.give_from(mine.astype(LOW)), spot)
            got = got.reshape(cores, local, count // cores, wide)
            other = line_k.swap(pick(got, 1 - core), 1)
            return settle([pick(got, core), other], core, 1).reshape(local, count, wide).astype(F32)

        weighted = (hidden_low.astype(F32) * gate).astype(LOW)
        grad_edown = deliver(dot(weighted.T, dy_slots), *expert_down.shape[:2])
        grad_egate = deliver(dot(second_slots.T, grad_a), *expert_gate.shape[:2])
        grad_eup = deliver(dot(second_slots.T, grad_b), *expert_up.shape[:2])

        def deliver_shared(grad):
            lead, _, count, wide = grad.shape
            grad = grad.reshape(lead, cores, blocks, count, wide)
            mine = total([pick(grad, core, 1), line_k.swap(pick(grad, 1 - core, 1), 1)])
            return total(line_t.give_from(mine.astype(LOW), 1))

        grad_sdown = dot(shared_low.T, dy_col).astype(LOW)
        grad_sdown = deliver_shared(grad_sdown.reshape(1, cores * blocks, -1, width))[0]
        grad_sin = dot(second_col.T, dsab).astype(LOW)
        grad_sin = deliver_shared(grad_sin.reshape(columns, cores * blocks, part, 2 * hidden))
        grad_sin = settle(line_z.give_from(grad_sin.astype(LOW)), col).transpose(1, 0, 2)
        grad_sgate = grad_sin[:, :, :hidden].reshape(part, -1).astype(F32)
        grad_sup = grad_sin[:, :, hidden:].reshape(part, -1).astype(F32)

        grad_outmat = lax.psum_scatter(grad_outmat, (Z, K), scatter_dimension=0, tiled=True)
        back = [(there, here) for here, there in move]
        grad_outmat = lax.ppermute(grad_outmat, (Z, K, C, D), back).astype(F32)
        grad_qkv = lax.psum_scatter(grad_qkv, (Z, K), scatter_dimension=0, tiled=True)
        grad_qkv = settle(line_t.give_from(grad_qkv.reshape(blocks, part, 3 * span)), blk)
        grad_qkv = grad_qkv.reshape(blocks, part, 3, span).transpose(2, 1, 0, 3)
        grad_qkv = grad_qkv.reshape(3, part, width).astype(F32)

        sums = jnp.concatenate([grad_router_t, grad_gain_first, grad_gain_second], axis=0)
        sums = sums.reshape(experts + 2, owners, blocks, part).transpose(2, 1, 0, 3)
        sums = total(line_t.give_from(sums))
        sums = total(line_e.give_from(sums))

        return (
            layer_out[None],
            grad_inputs[None],
            sums[experts],
            grad_qkv[0],
            grad_qkv[1],
            grad_qkv[2],
            grad_outmat,
            sums[experts + 1],
            sums[:experts].T,
            grad_sgate,
            grad_sup,
            grad_sdown,
            grad_egate,
            grad_eup,
            grad_edown,
        )

    return body


def solution(mesh):
    owners, blocks, halves = mesh.devices.shape
    mesh = Mesh(mesh.devices.reshape(owners // 2, 2, blocks, halves), (Z, K, C, D))
    every = P((Z, K, C, D))
    tokens = P((Z, K), (C, D))
    return jax.shard_map(
        make_body(mesh),
        mesh=mesh,
        in_specs=(tokens, P((Z, K)), tokens) + (every,) * 10 + (tokens,) * 4,
        out_specs=(tokens, tokens) + (every,) * 10 + (tokens,) * 3,
        check_vma=False,
    )
```

```python
import math

import jax
import jax.numpy as jnp
from jax import lax
from jax.sharding import Mesh
from jax.sharding import PartitionSpec as P

HD = 128
TOP = 6
EPS = 1e-06
MASKED = -1e30
Z, K, C, D = "z", "core", "context", "dp"
F32 = jnp.float32
LOW = jnp.bfloat16


class Line:
    def __init__(self, mesh, *names):
        self.names = names
        self.size = math.prod(mesh.shape[name] for name in names)

    def at(self):
        return lax.axis_index(self.names)

    def swap(self, value, delta):
        return lax.ppermute(value, self.names, [(i, i ^ delta) for i in range(self.size)])

    def share(self, value):
        return [value] + [self.swap(value, delta) for delta in range(1, self.size)]

    def give(self, pieces):
        return [pieces[0]] + [self.swap(pieces[delta], delta) for delta in range(1, self.size)]

    def give_from(self, stack, dim=0):
        here = self.at()
        return self.give([pick(stack, here ^ delta, dim) for delta in range(self.size)])

    def trade(self, blocks):
        return lax.all_to_all(blocks, self.names, split_axis=0, concat_axis=0, tiled=True)


def pick(stack, index, dim=0):
    return lax.dynamic_index_in_dim(stack, index, dim, keepdims=False)


def settle(pieces, index, dim=0):
    shape = list(pieces[0].shape)
    shape.insert(dim, len(pieces))
    out = jnp.zeros(shape, pieces[0].dtype)
    for delta, piece in enumerate(pieces):
        out = lax.dynamic_update_index_in_dim(out, piece, index ^ delta, dim)
    return out


def in_order(first, mine, other):
    return jnp.where(first, mine, other), jnp.where(first, other, mine)


def after(value, *events):
    return lax.optimization_barrier((value, *events))[0]


def dot(left, right):
    return jnp.dot(left, right, preferred_element_type=F32)


def total(pieces):
    out = pieces[0].astype(F32)
    for piece in pieces[1:]:
        out = out + piece.astype(F32)
    return out


def turn(values, cosine, sine, sign):
    half = HD // 2
    first, second = values[..., :half], values[..., half:]
    return jnp.concatenate(
        [first * cosine - sign * second * sine, second * cosine + sign * first * sine], axis=-1
    )


def norm_back(grad_normed, normed, scale, gain):
    scaled = grad_normed * gain
    return scale * (scaled - normed * jnp.mean(scaled * normed, axis=1, keepdims=True))


def swish_slope(values, sigma):
    return sigma * (1.0 + values * (1.0 - sigma))


def make_body(mesh):
    line_z, line_k, line_t = Line(mesh, Z), Line(mesh, K), Line(mesh, C, D)
    columns, cores, blocks = line_z.size, line_k.size, line_t.size
    owners = columns * cores

    def body(
        tokens_in,
        doc_ids,
        routes,
        gain_attn,
        w_query,
        w_key,
        w_value,
        w_out,
        gain_moe,
        w_router,
        shared_gate,
        shared_up,
        shared_down,
        expert_gate,
        expert_up,
        expert_down,
        cotangent,
    ):
        col, core, blk = line_z.at(), line_k.at(), line_t.at()
        x_low, dy_low = tokens_in[0], cotangent[0]
        rows, width = x_low.shape
        length = doc_ids.shape[1]
        part = w_query.shape[0]
        span = width // blocks
        heads = span // HD
        experts = w_router.shape[1]
        group = experts // columns
        line_s = line_t if blocks == group else Line(mesh, C)
        rest = () if blocks == group else (D,)
        spot = line_s.at()

        first = core == 0
        half = width // 2

        def column_halves(value):
            return in_order(first, value[..., :half], value[..., half:])

        def side_by_side(mine, other):
            return jnp.concatenate(in_order(first, mine, other), axis=-1)

        def both_cores(mine, other):
            return jnp.concatenate(in_order(first, mine, line_k.swap(other, 1)), axis=0)

        def all_rows(whole):
            if rest:
                whole = lax.all_gather(whole, rest, axis=1, tiled=True)
            return whole.reshape(-1, whole.shape[-1])

        down_part = both_cores(*column_halves(expert_down))
        in_part = both_cores(*in_order(first, expert_gate, expert_up))

        small = jnp.concatenate([w_router, gain_attn[:, None], gain_moe[:, None]], axis=1)
        small = jnp.pad(small, ((0, 0), (0, -small.shape[1] % 128)))
        extra = small.shape[1]
        mixed_in = jnp.concatenate(
            [w.reshape(part, blocks, span) for w in (w_query, w_key, w_value)]
            + [jnp.broadcast_to(small[:, None], (part, blocks, extra))],
            axis=2,
        ).transpose(1, 0, 2)
        move = [(i, (i % owners) * blocks + i // owners) for i in range(owners * blocks)]
        out_part = lax.ppermute(w_out, (Z, K, C, D), move)
        out_part = out_part.reshape(part, blocks, span).transpose(1, 0, 2)
        attn_part = settle(line_t.give_from(mixed_in), blk)
        attn_part = jnp.concatenate([attn_part, out_part], axis=2).reshape(blocks * part, -1)
        attn_mat = lax.all_gather(attn_part, (Z, K), axis=0, tiled=True)
        dy_col = lax.all_gather(after(dy_low, attn_mat), Z, axis=0, tiled=True)

        x_all = jnp.concatenate(line_t.share(x_low), axis=0).astype(F32)
        down_got = line_s.trade(down_part)
        in_got = line_s.trade(after(in_part, down_got))
        attn_mat = after(attn_mat, down_got)
        qkv = attn_mat[:, : 3 * span]
        small = attn_mat[:, 3 * span : 3 * span + extra].T
        router_t = small[:experts]
        gain_first = small[experts].astype(F32)[None]
        gain_second = small[experts + 1].astype(F32)[None]
        out_mat = attn_mat[:, 3 * span + extra :].reshape(owners, blocks, part, span)
        out_mat = out_mat.transpose(0, 2, 1, 3).reshape(owners * part, width)

        doc_row = doc_ids[0]
        order = blk ^ jnp.arange(blocks, dtype=jnp.int32)
        doc_starts = jnp.sum((doc_row[None, :] < doc_row[:, None]).astype(jnp.int32), axis=1)
        offsets = jnp.arange(length, dtype=jnp.int32) - doc_starts

        def reorder(row):
            grid = row.reshape(blocks, rows)
            return jnp.concatenate([pick(grid, order[i]) for i in range(blocks)])

        doc_here, off_here = reorder(doc_row), reorder(offsets)
        place = reorder(jnp.arange(length, dtype=jnp.int32))
        frequency = jnp.exp(
            jnp.arange(HD // 2, dtype=F32) * (-math.log(10000.0) / (HD // 2))
        )
        angles = off_here.astype(F32)[:, None] * frequency[None, :]
        cosine, sine = jnp.cos(angles)[:, None, :], jnp.sin(angles)[:, None, :]
        allowed = (place[:, None] >= place[None, :]) & (doc_here[:, None] == doc_here[None, :])

        first_scale = lax.rsqrt(jnp.mean(x_all * x_all, axis=1, keepdims=True) + EPS)
        first_normed = x_all * first_scale
        normed_low = (first_normed * gain_first).astype(LOW)
        made = dot(normed_low, qkv)
        routes_col = settle(line_z.share(after(routes[0], made)), col)

        def per_head(values):
            return values.reshape(length, heads, HD)

        query_low = turn(per_head(made[:, :span]), cosine, sine, 1.0).astype(LOW)
        key_low = turn(per_head(made[:, span : 2 * span]), cosine, sine, 1.0).astype(LOW)
        value_low = per_head(made[:, 2 * span :].astype(LOW))
        score_scale = HD ** (-0.5)
        scores = jnp.einsum("qhd,khd->hqk", query_low, key_low, preferred_element_type=F32)
        scores = jnp.where(allowed[None], scores * score_scale, MASKED)
        exponent = jnp.exp(scores - jnp.max(scores, axis=2, keepdims=True))
        attn_probs = exponent / jnp.sum(exponent, axis=2, keepdims=True)
        probs_low = attn_probs.astype(LOW)
        mixed_low = (
            jnp.einsum("hqk,khd->qhd", probs_low, value_low, preferred_element_type=F32)
            .astype(LOW)
            .reshape(length, span)
        )
        attn_out = dot(mixed_low, out_mat).astype(LOW).reshape(blocks, rows, width)
        in_got = after(in_got, attn_out)
        inputs = after(x_low, in_got).astype(F32)
        after_attn = inputs + total(line_t.give([attn_out[i] for i in range(blocks)]))

        second_scale = lax.rsqrt(jnp.mean(after_attn * after_attn, axis=1, keepdims=True) + EPS)
        second_normed = after_attn * second_scale
        second_low = (second_normed * gain_second).astype(LOW)
        second_col = lax.all_gather(second_low, Z, axis=0, tiled=True)
        hidden = shared_gate.shape[1] // columns
        shared_in = jnp.concatenate(
            [w.reshape(part, columns, hidden).transpose(1, 0, 2) for w in (shared_gate, shared_up)],
            axis=2,
        )
        shared_in = line_z.trade(after(shared_in, second_low))
        mat_down = all_rows(after(down_got, second_low))
        mat_down = side_by_side(mat_down, line_k.swap(mat_down, 1))
        mat_mine = all_rows(after(in_got, second_low))
        mat_other = line_k.swap(mat_mine, 1)

        def router(values):
            return jax.nn.softmax(dot(values, router_t.T), axis=1)

        router_probs = router(second_low)
        probs_col = router(second_col)

        capacity = min(rows, rows * TOP * 4 // (3 * experts))
        slots = columns * capacity
        wanted = col * group + (spot ^ jnp.arange(group, dtype=jnp.int32))
        hits = jnp.any(routes_col[None] == wanted[:, None, None, None], axis=3)
        ranks = jnp.cumsum(hits.astype(jnp.int32), axis=2) - 1
        ranks = jnp.where(hits, ranks, -1)
        chosen = ranks[:, :, None, :] == jnp.arange(capacity, dtype=jnp.int32)[:, None]
        same = jnp.eye(columns, dtype=jnp.bool_)[None, :, None, :, None]
        spread = (
            (chosen[:, :, :, None, :] & same).reshape(group * slots, columns * rows).astype(LOW)
        )

        def dispatch(values):
            sent = dot(spread, values).astype(LOW).reshape(group, slots, width)
            return jnp.concatenate(line_s.give([sent[i] for i in range(group)]), axis=0)

        def collect(values):
            parts = values.reshape(group, slots, width)
            back = line_s.give([parts[i] for i in range(group)])
            return jnp.concatenate(back, axis=0)

        dy_slots = dispatch(dy_col)
        du_raw = dot(dy_slots, mat_down.T)
        gate_col = jnp.sum(
            jnp.where(
                jnp.arange(experts, dtype=jnp.int32) == wanted[:, None, None], probs_col[None], 0.0
            ),
            axis=2,
        ).reshape(group, columns, 1, rows)
        gate_sent = jnp.sum(jnp.where(chosen, gate_col, 0.0), axis=3).reshape(group, 1, slots)
        gate = jnp.concatenate(line_s.give([gate_sent[i] for i in range(group)]), axis=1)
        gate = gate.reshape(group * slots, 1)

        second_slots = after(dispatch(after(second_col, dy_slots)), du_raw)
        made_mine, made_other = dot(second_slots, mat_mine), dot(second_slots, mat_other)
        pre_gate = jnp.where(first, made_mine, made_other)
        pre_up = jnp.where(first, made_other, made_mine)
        sigma = jax.nn.sigmoid(pre_gate)
        hidden_low = (pre_gate * sigma * pre_up).astype(LOW)
        dgate = jnp.sum(hidden_low.astype(F32) * du_raw, axis=1)
        du = du_raw * gate
        grad_a = (du * pre_up * swish_slope(pre_gate, sigma)).astype(LOW)
        grad_b = (du * pre_gate * sigma).astype(LOW)
        grad_mine = jnp.where(first, grad_a, grad_b)
        grad_other = jnp.where(first, grad_b, grad_a)
        grad_slots = (dot(grad_mine, mat_mine.T) + dot(grad_other, mat_other.T)).astype(LOW)

        mat_sin, mat_sdown = after((shared_in, shared_down), second_slots)
        mat_sin = lax.all_gather(mat_sin, (K, C, D), axis=1, tiled=True)
        mat_sin = mat_sin.reshape(width, 2 * hidden)
        mat_sdown = lax.all_gather(mat_sdown, (K, C, D), axis=0, tiled=True)
        second_late, dy_late = after((second_col, dy_col), grad_slots)
        shared_pre = dot(second_late, mat_sin)
        shared_a, shared_b = shared_pre[:, :hidden], shared_pre[:, hidden:]
        shared_sigma = jax.nn.sigmoid(shared_a)
        shared_low = (shared_a * shared_sigma * shared_b).astype(LOW)
        dsu = dot(dy_late, mat_sdown.T)
        dsa = (dsu * shared_b * swish_slope(shared_a, shared_sigma)).astype(LOW)
        dsb = (dsu * shared_a * shared_sigma).astype(LOW)
        dsab = jnp.concatenate([dsa, dsb], axis=1)

        grad_routed = dot(spread.T, after(collect(grad_slots), dsab))
        grad_second = dot(dsab, mat_sin.T) + grad_routed
        grad_second = lax.psum_scatter(
            grad_second.astype(LOW), Z, scatter_dimension=0, tiled=True
        )

        dgate_parts = dgate.reshape(group, 1, slots)
        dgate_back = line_s.give([dgate_parts[i] for i in range(group)])
        dgate_back = jnp.stack(dgate_back).reshape(group, columns, capacity, 1)
        dgate_col = jnp.sum(jnp.where(chosen, dgate_back, 0.0), axis=2)
        dgate_col = settle([dgate_col[i] for i in range(group)], spot)
        dprobs = settle(line_z.give_from(dgate_col.transpose(1, 0, 2)), col)
        dprobs = dprobs.reshape(experts, rows).T
        dlogits = (
            router_probs * (dprobs - jnp.sum(dprobs * router_probs, axis=1, keepdims=True))
        ).astype(LOW)
        grad_router_t = dot(dlogits.T, second_low)
        grad_second = grad_second.astype(F32) + dot(dlogits, router_t)

        grad_gain_second = jnp.sum(grad_second * second_normed, axis=0, keepdims=True)
        dy = dy_low.astype(F32)
        grad_after = dy + norm_back(grad_second, second_normed, second_scale, gain_second)
        grad_after_low = jnp.concatenate(line_t.share(grad_after.astype(LOW)), axis=0)

        grad_mixed = per_head(dot(grad_after_low, out_mat.T).astype(LOW))
        grad_outmat = dot(mixed_low.T, grad_after_low).astype(LOW)
        grad_probs = jnp.einsum("qhd,khd->hqk", grad_mixed, value_low, preferred_element_type=F32)
        grad_value = jnp.einsum("hqk,qhd->khd", probs_low, grad_mixed, preferred_element_type=F32)
        grad_scores = (
            attn_probs * (grad_probs - jnp.sum(grad_probs * attn_probs, axis=2, keepdims=True))
        ).astype(LOW)
        grad_query = jnp.einsum("hqk,khd->qhd", grad_scores, key_low, preferred_element_type=F32)
        grad_key = jnp.einsum("hqk,qhd->khd", grad_scores, query_low, preferred_element_type=F32)
        grad_query = turn(grad_query * score_scale, cosine, sine, -1.0)
        grad_key = turn(grad_key * score_scale, cosine, sine, -1.0)
        grad_made = jnp.concatenate(
            [g.astype(LOW).reshape(length, span) for g in (grad_query, grad_key, grad_value)], axis=1
        )
        grad_qkv = dot(normed_low.T, grad_made).astype(LOW)
        grad_first = dot(grad_made, qkv.T).astype(LOW).reshape(blocks, rows, width)
        grad_first = total(line_t.give([grad_first[i] for i in range(blocks)]))
        local_normed = first_normed[:rows]
        grad_gain_first = jnp.sum(grad_first * local_normed, axis=0, keepdims=True)
        grad_inputs = grad_after + norm_back(
            grad_first, local_normed, first_scale[:rows], gain_first
        )

        routed = (dot(after(hidden_low, grad_slots), mat_down) * gate).astype(LOW)
        layer_out = dot(shared_low, mat_sdown) + dot(spread.T, collect(after(routed, grad_routed)))
        layer_out = lax.psum_scatter(layer_out.astype(LOW), Z, scatter_dimension=0, tiled=True)
        layer_out = after_attn + layer_out.astype(F32)

        def send_home(mine, other):
            mine = total([mine, line_k.swap(other, 1)]).astype(LOW)
            mine = mine.reshape(line_s.size, -1, mine.shape[-1])
            if rest:
                mine = lax.psum_scatter(mine, rest, scatter_dimension=1, tiled=True)
            return line_s.trade(mine)

        def home(got):
            got = got.reshape(cores, -1, *got.shape[1:])
            kept, other = in_order(first, got[0], got[1])
            return kept, line_k.swap(other, 1)

        weighted = (hidden_low.astype(F32) * gate).astype(LOW)
        grad_down = dot(after(weighted, grad_slots).T, dy_slots).astype(LOW)
        down_back = send_home(*column_halves(grad_down))
        slots_late = after(second_slots, grad_slots)
        in_back = send_home(
            dot(slots_late.T, grad_mine).astype(LOW), dot(slots_late.T, grad_other).astype(LOW)
        )

        def shared_home(grad):
            lead, count, wide = grad.shape
            count = count // (cores * blocks)
            grad = grad.astype(LOW).reshape(lead, cores, blocks * count, wide)
            mine, other = in_order(first, grad[:, 0], grad[:, 1])
            mine = total([mine, line_k.swap(other, 1)]).astype(LOW)
            return line_t.trade(mine.reshape(lead, blocks, count, wide).transpose(1, 0, 2, 3))

        sdown_back = shared_home(dot(shared_low.T, dy_late)[None])
        sin_back = shared_home(
            dot(second_late.T, dsab).reshape(columns, cores * blocks * part, 2 * hidden)
        )

        down_back, in_back, sdown_back, sin_back = after(
            (down_back, in_back, sdown_back, sin_back), grad_made
        )
        grad_edown = side_by_side(*home(down_back)).astype(F32)
        kept, came = home(in_back)
        grad_egate = jnp.where(first, kept, came).astype(F32)
        grad_eup = jnp.where(first, came, kept).astype(F32)
        grad_sdown = total([sdown_back[i, 0] for i in range(blocks)])
        grad_sin = total([sin_back[i] for i in range(blocks)]).astype(LOW)
        grad_sin = line_z.trade(grad_sin).transpose(1, 0, 2).astype(F32)
        grad_sgate = grad_sin[:, :, :hidden].reshape(part, -1)
        grad_sup = grad_sin[:, :, hidden:].reshape(part, -1)

        grad_outmat = lax.psum_scatter(grad_outmat, (Z, K), scatter_dimension=0, tiled=True)
        back = [(there, here) for here, there in move]
        grad_outmat = lax.ppermute(grad_outmat, (Z, K, C, D), back).astype(F32)
        grad_qkv = lax.psum_scatter(grad_qkv, (Z, K), scatter_dimension=0, tiled=True)
        grad_qkv = line_t.trade(grad_qkv.reshape(blocks, part, 3 * span))
        grad_qkv = grad_qkv.reshape(blocks, part, 3, span).transpose(2, 1, 0, 3)
        grad_qkv = grad_qkv.reshape(3, part, width).astype(F32)

        sums = jnp.concatenate([grad_router_t, grad_gain_first, grad_gain_second], axis=0)
        sums = sums.reshape(experts + 2, columns, cores, blocks, part).transpose(3, 2, 1, 0, 4)
        sums = total(line_t.give_from(sums))
        sums = total(line_k.give_from(sums))
        sums = total(line_z.give_from(sums))

        return (
            layer_out[None],
            grad_inputs[None],
            sums[experts],
            grad_qkv[0],
            grad_qkv[1],
            grad_qkv[2],
            grad_outmat,
            sums[experts + 1],
            sums[:experts].T,
            grad_sgate,
            grad_sup,
            grad_sdown,
            grad_egate,
            grad_eup,
            grad_edown,
        )

    return body


def solution(mesh):
    owners, blocks, halves = mesh.devices.shape
    mesh = Mesh(mesh.devices.reshape(owners // 2, 2, blocks, halves), (Z, K, C, D))
    every = P((Z, K, C, D))
    tokens = P((Z, K), (C, D))
    return jax.shard_map(
        make_body(mesh),
        mesh=mesh,
        in_specs=(tokens, P((Z, K)), tokens) + (every,) * 10 + (tokens,) * 4,
        out_specs=(tokens, tokens) + (every,) * 10 + (tokens,) * 3,
        check_vma=False,
    )
```

```python
import math

import jax
import jax.numpy as jnp
from jax import lax
from jax.experimental import pallas as pl
from jax.experimental.pallas import tpu as pltpu
from jax.sharding import Mesh
from jax.sharding import PartitionSpec as P

HD = 128
TOP = 6
EPS = 1e-06
MASKED = -1e30
Z, K, C, D = "z", "core", "context", "dp"
F32 = jnp.float32
LOW = jnp.bfloat16


class Line:
    def __init__(self, mesh, *names):
        self.names = names
        self.size = math.prod(mesh.shape[name] for name in names)

    def at(self):
        return lax.axis_index(self.names)

    def swap(self, value, delta):
        return lax.ppermute(value, self.names, [(i, i ^ delta) for i in range(self.size)])

    def share(self, value):
        return [value] + [self.swap(value, delta) for delta in range(1, self.size)]

    def give(self, pieces):
        return [pieces[0]] + [self.swap(pieces[delta], delta) for delta in range(1, self.size)]

    def give_from(self, stack, dim=0):
        here = self.at()
        return self.give([pick(stack, here ^ delta, dim) for delta in range(self.size)])

    def trade(self, blocks):
        return lax.all_to_all(blocks, self.names, split_axis=0, concat_axis=0, tiled=True)


def pick(stack, index, dim=0):
    return lax.dynamic_index_in_dim(stack, index, dim, keepdims=False)


def settle(pieces, index, dim=0):
    shape = list(pieces[0].shape)
    shape.insert(dim, len(pieces))
    out = jnp.zeros(shape, pieces[0].dtype)
    for delta, piece in enumerate(pieces):
        out = lax.dynamic_update_index_in_dim(out, piece, index ^ delta, dim)
    return out


def in_order(first, mine, other):
    return jnp.where(first, mine, other), jnp.where(first, other, mine)


def after(value, *events):
    return lax.optimization_barrier((value, *events))[0]


def dot(left, right):
    return jnp.dot(left, right, preferred_element_type=F32)


def total(pieces):
    out = pieces[0].astype(F32)
    for piece in pieces[1:]:
        out = out + piece.astype(F32)
    return out


def norm_back(grad_normed, normed, scale, gain):
    scaled = grad_normed * gain
    return scale * (scaled - normed * jnp.mean(scaled * normed, axis=1, keepdims=True))


def swish_slope(values, sigma):
    return sigma * (1.0 + values * (1.0 - sigma))


def whole_spec(array):
    return pl.BlockSpec(array.shape, lambda j: (0,) * array.ndim)


def attention_probs(query, key, places, docs, places_row, docs_row):
    across = (((1,), (1,)), ((), ()))
    scores = lax.dot_general(query, key, across, preferred_element_type=F32) * HD ** (-0.5)
    allowed = (places >= places_row) & (docs == docs_row)
    scores = jnp.where(allowed, scores, MASKED)
    exponent = jnp.exp(scores - jnp.max(scores, axis=1, keepdims=True))
    return exponent / jnp.sum(exponent, axis=1, keepdims=True)


def attention_kernel(
    normed, w_q, w_k, w_v, w_o, cosine, sine, places, docs, places_row, docs_row,
    query, key, value, mixed, out, sums,
):
    step = pl.program_id(0)
    weights = jnp.concatenate([w_q[...], w_k[...], w_v[...]], axis=1)
    made = jnp.dot(normed[...], weights, preferred_element_type=F32)

    def rotated(values):
        swapped = pltpu.roll(values, HD // 2, axis=1)
        return (values * cosine[...] + swapped * sine[...]).astype(LOW)

    query[...] = rotated(made[:, :HD])
    key[...] = rotated(made[:, HD : 2 * HD])
    value[...] = made[:, 2 * HD :].astype(LOW)
    probs = attention_probs(
        query[...], key[...], places[...], docs[...], places_row[...], docs_row[...]
    )
    low = jnp.dot(probs.astype(LOW), value[...], preferred_element_type=F32).astype(LOW)
    mixed[...] = low
    part = jnp.dot(low, w_o[...], preferred_element_type=F32)

    @pl.when(step == 0)
    def _():
        sums[...] = part

    @pl.when(step > 0)
    def _():
        sums[...] += part

    @pl.when(step == pl.num_programs(0) - 1)
    def _():
        out[...] = sums[...].astype(LOW)


def attention_forward(normed, mats, out_mat, tables):
    length, width = normed.shape
    span = out_mat.shape[0]
    heads = span // HD
    head = lambda rows, first: pl.BlockSpec((rows, HD), lambda j: (0, first + j))
    shapes = [jax.ShapeDtypeStruct((length, span), LOW)] * 4
    shapes.append(jax.ShapeDtypeStruct((length, width), LOW))
    return pl.pallas_call(
        attention_kernel,
        grid=(heads,),
        in_specs=[
            whole_spec(normed),
            head(width, 0),
            head(width, heads),
            head(width, 2 * heads),
            pl.BlockSpec((HD, width), lambda j: (j, 0)),
        ]
        + [whole_spec(table) for table in tables],
        out_specs=[head(length, 0)] * 4 + [whole_spec(shapes[4])],
        out_shape=shapes,
        scratch_shapes=[pltpu.VMEM((length, width), F32)],
        compiler_params=pltpu.CompilerParams(vmem_limit_bytes=48 * 2**20),
        cost_estimate=pl.CostEstimate(
            flops=2 * length * span * (4 * width + 2 * length),
            bytes_accessed=2 * (2 * length * width + 4 * width * span + 4 * length * span),
            transcendentals=heads * length * length,
        ),
    )(normed, mats, mats, mats, out_mat, *tables)


def attention_back_kernel(
    grad_out, w_o, query, key, value, mixed, cosine, sine, places, docs, places_row, docs_row,
    grads, grad_w,
):
    step = pl.program_id(0)
    heads = (grads.shape[1] - 1) // (3 * HD)
    across = (((1,), (1,)), ((), ()))
    down = (((0,), (0,)), ((), ()))
    given = grad_out[...]
    grad_w[...] = lax.dot_general(mixed[...], given, down, preferred_element_type=F32).astype(LOW)
    low = lax.dot_general(given, w_o[...], across, preferred_element_type=F32).astype(LOW)
    probs = attention_probs(
        query[...], key[...], places[...], docs[...], places_row[...], docs_row[...]
    )
    grad_p = lax.dot_general(low, value[...], across, preferred_element_type=F32)
    grad_v = lax.dot_general(probs.astype(LOW), low, down, preferred_element_type=F32)
    grad_s = probs * (grad_p - jnp.sum(grad_p * probs, axis=1, keepdims=True))
    grad_s = grad_s.astype(LOW)
    scale = HD ** (-0.5)
    grad_q = jnp.dot(grad_s, key[...], preferred_element_type=F32) * scale
    grad_k = lax.dot_general(grad_s, query[...], down, preferred_element_type=F32) * scale

    def unrotated(values):
        swapped = pltpu.roll(values, HD // 2, axis=1)
        return (values * cosine[...] - swapped * sine[...]).astype(LOW)

    def column(first):
        return pl.ds(pl.multiple_of((first * heads + step) * HD, HD), HD)

    grads[:, column(0)] = unrotated(grad_q)
    grads[:, column(1)] = unrotated(grad_k)
    grads[:, column(2)] = grad_v.astype(LOW)

    @pl.when(step == 0)
    def _():
        rest = grads.shape[1] - 3 * HD * heads
        grads[:, 3 * HD * heads :] = jnp.zeros((grads.shape[0], rest), LOW)


def attention_back(grad_out, out_mat, kept, tables, extra):
    length, width = grad_out.shape
    span = out_mat.shape[0]
    heads = span // HD
    head = pl.BlockSpec((length, HD), lambda j: (0, j))
    row = pl.BlockSpec((HD, width), lambda j: (j, 0))
    shapes = [
        jax.ShapeDtypeStruct((length, 3 * span + extra), LOW),
        jax.ShapeDtypeStruct((span, width), LOW),
    ]

    return pl.pallas_call(
        attention_back_kernel,
        grid=(heads,),
        in_specs=[whole_spec(grad_out), row] + [head] * 4 + [whole_spec(t) for t in tables],
        out_specs=[whole_spec(shapes[0]), row],
        out_shape=shapes,
        compiler_params=pltpu.CompilerParams(vmem_limit_bytes=48 * 2**20),
        cost_estimate=pl.CostEstimate(
            flops=2 * length * span * (2 * width + 5 * length),
            bytes_accessed=2 * (length * width + 2 * width * span + 7 * length * span),
            transcendentals=heads * length * length,
        ),
    )(grad_out, out_mat, *kept, *tables)


def expert_kernel(flag, slots, mine, other, raw, gate, hidden, grads, dgate):
    step = pl.program_id(0)
    tile = mine.shape[1]
    wide = grads.shape[1] // 2
    is_first = flag[0] == 1
    weights = jnp.concatenate([mine[...], other[...]], axis=1)
    count = slots.shape[0]
    chunk = min(count, 256)
    left_at = pl.multiple_of(step * tile, tile)
    right_at = pl.multiple_of(wide + step * tile, tile)
    for at in range(0, count, chunk):
        here = slice(at, at + chunk)
        made = jnp.dot(slots[here, :], weights, preferred_element_type=F32)
        left, right = made[:, :tile], made[:, tile:]
        a = jnp.where(is_first, left, right)
        b = jnp.where(is_first, right, left)
        sigma = jax.nn.sigmoid(a)
        silu = a * sigma
        low = (silu * b).astype(LOW)
        hidden[here, :] = low
        du = raw[here, :]
        part = jnp.sum(low.astype(F32) * du, axis=1, keepdims=True)
        du = du * gate[here, :]
        da = du * b * (sigma * (1.0 + a * (1.0 - sigma)))
        db = du * silu
        grads[here, pl.ds(left_at, tile)] = jnp.where(is_first, da, db).astype(LOW)
        grads[here, pl.ds(right_at, tile)] = jnp.where(is_first, db, da).astype(LOW)
        dgate[here, :] = part + jnp.where(step == 0, 0.0, dgate[here, :])


def expert_forward(flag, slots, mine, other, raw, gate):
    count, width = slots.shape
    wide = mine.shape[1]
    tile = 128
    column = lambda rows: pl.BlockSpec((rows, tile), lambda j: (0, j))
    shapes = (
        jax.ShapeDtypeStruct((count, wide), LOW),
        jax.ShapeDtypeStruct((count, 2 * wide), LOW),
        jax.ShapeDtypeStruct((count, 1), F32),
    )
    return pl.pallas_call(
        expert_kernel,
        grid=(wide // tile,),
        in_specs=[
            pl.BlockSpec(memory_space=pltpu.SMEM),
            whole_spec(slots),
            column(width),
            column(width),
            column(count),
            whole_spec(gate),
        ],
        out_specs=(column(count), whole_spec(shapes[1]), whole_spec(shapes[2])),
        out_shape=shapes,
        compiler_params=pltpu.CompilerParams(vmem_limit_bytes=48 * 2**20),
        cost_estimate=pl.CostEstimate(
            flops=4 * count * width * wide,
            bytes_accessed=2 * (count * width + 2 * width * wide + 5 * count * wide),
            transcendentals=count * wide,
        ),
    )(flag, slots, mine, other, raw, gate)


def back_kernel(flag, grads, mine, other, dgate, out):
    step = pl.program_id(0)
    tile = mine.shape[0]
    wide = grads.shape[1] // 2
    width = out.shape[1] - 128
    across = (((1,), (1,)), ((), ()))
    made = lax.dot_general(grads[:, :wide], mine[...], across, preferred_element_type=F32)
    made += lax.dot_general(grads[:, wide:], other[...], across, preferred_element_type=F32)
    out[:, pl.ds(pl.multiple_of(step * tile, tile), tile)] = made.astype(LOW)

    @pl.when(step == 0)
    def _():
        lanes = lax.broadcasted_iota(jnp.int32, (out.shape[0], 128), 1)
        high = dgate[...].astype(LOW).astype(F32)
        rest = dgate[...] - high
        cols = jnp.where(lanes == flag[1], high, jnp.where(lanes == flag[1] + 64, rest, 0.0))
        out[:, width:] = cols.astype(LOW)


def expert_back(flag, grads, mine, other, dgate):
    count = grads.shape[0]
    width, wide = mine.shape
    tile = 256
    shape = jax.ShapeDtypeStruct((count, width + 128), LOW)
    row = pl.BlockSpec((tile, wide), lambda j: (j, 0))
    return pl.pallas_call(
        back_kernel,
        grid=(width // tile,),
        in_specs=[
            pl.BlockSpec(memory_space=pltpu.SMEM),
            whole_spec(grads),
            row,
            row,
            whole_spec(dgate),
        ],
        out_specs=whole_spec(shape),
        out_shape=shape,
        compiler_params=pltpu.CompilerParams(vmem_limit_bytes=48 * 2**20),
        cost_estimate=pl.CostEstimate(
            flops=4 * count * width * wide,
            bytes_accessed=2 * (2 * count * wide + 2 * width * wide + count * width),
            transcendentals=0,
        ),
    )(flag, grads, mine, other, dgate)


def make_body(mesh):
    line_z, line_k, line_t = Line(mesh, Z), Line(mesh, K), Line(mesh, C, D)
    columns, cores, blocks = line_z.size, line_k.size, line_t.size
    owners = columns * cores

    def body(
        tokens_in,
        doc_ids,
        routes,
        gain_attn,
        w_query,
        w_key,
        w_value,
        w_out,
        gain_moe,
        w_router,
        shared_gate,
        shared_up,
        shared_down,
        expert_gate,
        expert_up,
        expert_down,
        cotangent,
    ):
        col, core, blk = line_z.at(), line_k.at(), line_t.at()
        x_low, dy_low = tokens_in[0], cotangent[0]
        rows, width = x_low.shape
        length = doc_ids.shape[1]
        part = w_query.shape[0]
        span = width // blocks
        heads = span // HD
        experts = w_router.shape[1]
        group = experts // columns
        line_s = line_t if blocks == group else Line(mesh, C)
        rest = () if blocks == group else (D,)
        spot = line_s.at()

        first = core == 0
        half = width // 2

        def column_halves(value):
            return in_order(first, value[..., :half], value[..., half:])

        def side_by_side(mine, other):
            return jnp.concatenate(in_order(first, mine, other), axis=-1)

        def both_cores(mine, other):
            return jnp.concatenate(in_order(first, mine, line_k.swap(other, 1)), axis=0)

        def all_rows(whole):
            if rest:
                whole = lax.all_gather(whole, rest, axis=1, tiled=True)
            return whole.reshape(-1, whole.shape[-1])

        down_part = both_cores(*column_halves(expert_down))
        in_part = both_cores(*in_order(first, expert_gate, expert_up))

        small = jnp.concatenate([w_router, gain_attn[:, None], gain_moe[:, None]], axis=1)
        small = jnp.pad(small, ((0, 0), (0, -small.shape[1] % 128)))
        extra = small.shape[1]
        mixed_in = jnp.concatenate(
            [w.reshape(part, blocks, span) for w in (w_query, w_key, w_value)]
            + [jnp.broadcast_to(small[:, None], (part, blocks, extra))],
            axis=2,
        ).transpose(1, 0, 2)
        move = [(i, (i % owners) * blocks + i // owners) for i in range(owners * blocks)]
        out_part = lax.ppermute(w_out, (Z, K, C, D), move)
        out_part = out_part.reshape(part, blocks, span).transpose(1, 0, 2)
        attn_part = settle(line_t.give_from(mixed_in), blk)
        attn_part = jnp.concatenate([attn_part, out_part], axis=2).reshape(blocks * part, -1)
        attn_mat = lax.all_gather(attn_part, (Z, K), axis=0, tiled=True)
        dy_col = lax.all_gather(after(dy_low, attn_mat), Z, axis=0, tiled=True)

        x_got = line_t.share(x_low)
        down_got = line_s.trade(down_part)
        routes_got = line_z.share(routes[0])
        down_got, in_part, x_got, routes_got = lax.optimization_barrier(
            (down_got, in_part, x_got, routes_got)
        )
        in_got = line_s.trade(in_part)
        routes_col = settle(routes_got, col)
        x_all = jnp.concatenate(x_got, axis=0).astype(F32)
        small = attn_mat[:, 3 * span : 3 * span + extra].T
        router_t = small[:experts]
        gain_first = small[experts].astype(F32)[None]
        gain_second = small[experts + 1].astype(F32)[None]
        out_mat = attn_mat[:, 3 * span + extra :].reshape(owners, blocks, part, span)
        out_mat = out_mat.transpose(0, 2, 1, 3).reshape(owners * part, width)

        doc_row = doc_ids[0]
        order = blk ^ jnp.arange(blocks, dtype=jnp.int32)
        doc_starts = jnp.sum((doc_row[None, :] < doc_row[:, None]).astype(jnp.int32), axis=1)
        offsets = jnp.arange(length, dtype=jnp.int32) - doc_starts

        def reorder(row):
            grid = row.reshape(blocks, rows)
            return jnp.concatenate([pick(grid, order[i]) for i in range(blocks)])

        doc_here, off_here = reorder(doc_row), reorder(offsets)
        place = reorder(jnp.arange(length, dtype=jnp.int32))
        frequency = jnp.exp(
            jnp.arange(HD // 2, dtype=F32) * (-math.log(10000.0) / (HD // 2))
        )
        angles = off_here.astype(F32)[:, None] * frequency[None, :]
        cosine, sine = jnp.cos(angles), jnp.sin(angles)
        tables = (
            jnp.concatenate([cosine, cosine], axis=1),
            jnp.concatenate([-sine, sine], axis=1),
            place[:, None],
            doc_here[:, None],
            place[None, :],
            doc_here[None, :],
        )

        first_scale = lax.rsqrt(jnp.mean(x_all * x_all, axis=1, keepdims=True) + EPS)
        first_normed = x_all * first_scale
        normed_low = (first_normed * gain_first).astype(LOW)
        *kept, attn_out = attention_forward(normed_low, attn_mat, out_mat, tables)
        attn_out = attn_out.reshape(blocks, rows, width)

        hidden = shared_gate.shape[1] // columns
        shared_in = jnp.concatenate(
            [w.reshape(part, columns, hidden).transpose(1, 0, 2) for w in (shared_gate, shared_up)],
            axis=2,
        )

        in_got = after(in_got, attn_out)
        inputs = after(x_low, in_got).astype(F32)
        after_attn = inputs + total(line_t.give([attn_out[i] for i in range(blocks)]))

        second_scale = lax.rsqrt(jnp.mean(after_attn * after_attn, axis=1, keepdims=True) + EPS)
        second_normed = after_attn * second_scale
        second_low = (second_normed * gain_second).astype(LOW)
        second_col = lax.all_gather(second_low, Z, axis=0, tiled=True)
        mat_down = all_rows(after(down_got, second_low))
        mat_down = side_by_side(mat_down, line_k.swap(mat_down, 1))
        mat_mine = all_rows(after(in_got, second_low))
        mat_other = line_k.swap(mat_mine, 1)
        shared_in = settle(line_z.give_from(after(shared_in, second_col)), col)

        def router(values):
            return jax.nn.softmax(dot(values, router_t.T), axis=1)

        router_probs = router(second_low)

        capacity = min(rows, rows * TOP * 4 // (3 * experts))
        slots = columns * capacity
        wanted = col * group + jnp.arange(group, dtype=jnp.int32)
        hits = jnp.any(routes_col[None] == wanted[:, None, None, None], axis=3)
        ranks = jnp.cumsum(hits.astype(jnp.int32), axis=2) - 1
        ranks = jnp.where(hits, ranks, -1)
        chosen = ranks[:, :, None, :] == jnp.arange(capacity, dtype=jnp.int32)[:, None]
        same = jnp.eye(columns, dtype=jnp.bool_)[None, :, None, :, None]
        spread = (
            (chosen[:, :, :, None, :] & same).reshape(group * slots, columns * rows).astype(LOW)
        )

        def dispatch(values):
            sent = dot(spread, values).astype(LOW).reshape(group, slots, width)
            return line_s.trade(sent).reshape(group * slots, width)

        def collect(values):
            return line_s.trade(values.reshape(group, slots, -1)).reshape(group * slots, -1)

        dy_slots = dispatch(dy_col)
        du_raw = dot(dy_slots, mat_down.T)
        second_slots = after(dispatch(after(second_col, dy_slots)), du_raw, mat_other)
        expert = col * group + spot
        gate = lax.dynamic_slice_in_dim(router(second_slots), expert, 1, axis=1)
        flag = jnp.stack([first.astype(jnp.int32), expert])
        hidden_low, grad_in, dgate = expert_forward(
            flag, second_slots, mat_mine, mat_other, du_raw, gate
        )
        wide = hidden_low.shape[1]

        cuts = -(-width // (2 * hidden))
        down_cuts = jnp.pad(shared_down, ((0, 0), (0, cuts * 2 * hidden - width)))
        shared_part = jnp.concatenate(
            [shared_in.reshape(columns * part, 2 * hidden)] + jnp.split(down_cuts, cuts, axis=1)
        )
        shared_all = lax.all_gather(after(shared_part, second_slots), (K, C, D), axis=0)
        grad_slots = expert_back(flag, grad_in, mat_mine, mat_other, dgate)

        shared_all = after(shared_all, grad_slots)
        mat_sin = shared_all[:, : columns * part].reshape(-1, columns, part, 2 * hidden)
        mat_sin = mat_sin.transpose(1, 0, 2, 3).reshape(width, 2 * hidden)
        mat_sdown = jnp.concatenate(jnp.split(shared_all[:, columns * part :], cuts, axis=1), axis=2)
        mat_sdown = mat_sdown[:, :, :width].reshape(hidden, width)
        second_late, dy_late = after((second_col, dy_col), grad_slots)
        shared_pre = dot(second_late, mat_sin)
        shared_a, shared_b = shared_pre[:, :hidden], shared_pre[:, hidden:]
        shared_sigma = jax.nn.sigmoid(shared_a)
        shared_low = (shared_a * shared_sigma * shared_b).astype(LOW)
        dsu = dot(dy_late, mat_sdown.T)
        dsa = (dsu * shared_b * swish_slope(shared_a, shared_sigma)).astype(LOW)
        dsb = (dsu * shared_a * shared_sigma).astype(LOW)
        dsab = jnp.concatenate([dsa, dsb], axis=1)

        routed = (dot(after(hidden_low, dsab), mat_down) * gate).astype(LOW)
        def both_parts(mine, other):
            return [mine, line_k.swap(other, 1)]

        def low_total(pieces):
            return total(pieces).astype(LOW)

        def shared_home(grad):
            lead, count, wide = grad.shape
            grad = grad.reshape(lead, cores, count // cores, wide)
            return both_parts(*in_order(first, grad[:, 0], grad[:, 1]))

        def by_owner(mine):
            lead, count, wide = mine.shape
            return mine.reshape(lead, blocks, count // blocks, wide).transpose(1, 0, 2, 3)

        slots_back = collect(grad_slots)
        grad_routed = dot(spread.T, after(slots_back, routed))
        grad_second = jnp.concatenate(
            [dot(dsab, mat_sin.T) + grad_routed[:, :width], grad_routed[:, width:]], axis=1
        )
        second_sent = grad_second.astype(LOW)
        grad_second = lax.psum_scatter(second_sent, Z, scatter_dimension=0, tiled=True).astype(F32)


        def send_home(mine):
            mine = mine.reshape(line_s.size, -1, mine.shape[-1])
            if rest:
                mine = lax.psum_scatter(mine, rest, scatter_dimension=1, tiled=True)
            return mine

        def home(got):
            got = got.reshape(cores, -1, *got.shape[1:])
            kept, other = in_order(first, got[0], got[1])
            return kept, line_k.swap(other, 1)

        weighted = (hidden_low.astype(F32) * gate).astype(LOW)
        slots_late = after(second_slots, grad_slots)
        grad_w = dot(slots_late.T, grad_in).astype(LOW)

        routed_back = collect(after(routed, grad_routed))
        grad_sin = dot(second_late.T, dsab).astype(LOW)
        grad_down = dot(weighted.T, dy_slots).astype(LOW)
        down_sums = low_total(both_parts(*column_halves(grad_down)))
        sin_sums = shared_home(grad_sin.reshape(columns, cores * blocks * part, 2 * hidden))
        in_sums = both_parts(grad_w[:, :wide], grad_w[:, wide:])
        in_sums = low_total(in_sums)
        sin_sums = by_owner(low_total(sin_sums))
        layer_sent = (dot(shared_low, mat_sdown) + dot(spread.T, routed_back)).astype(LOW)
        down_back = line_s.trade(send_home(down_sums))
        layer_out = lax.psum_scatter(layer_sent, Z, scatter_dimension=0, tiled=True)
        grad_sdown = dot(shared_low.T, after(dy_late, second_sent)).astype(LOW)
        sdown_sums = by_owner(low_total(shared_home(grad_sdown[None])))

        dprobs = grad_second[:, width : width + experts]
        dprobs = dprobs + grad_second[:, width + 64 : width + 64 + experts]
        dlogits = (
            router_probs * (dprobs - jnp.sum(dprobs * router_probs, axis=1, keepdims=True))
        ).astype(LOW)
        grad_router_t = dot(dlogits.T, second_low)
        grad_second = grad_second[:, :width] + dot(dlogits, router_t)

        grad_gain_second = jnp.sum(grad_second * second_normed, axis=0, keepdims=True)
        dy = dy_low.astype(F32)
        grad_after = dy + norm_back(grad_second, second_normed, second_scale, gain_second)
        grad_after_low = grad_after.astype(LOW)
        grad_after_low = jnp.concatenate(line_t.share(grad_after_low), axis=0)
        in_back = line_s.trade(send_home(in_sums))
        sin_back = line_t.trade(sin_sums)

        grad_made, grad_outmat = attention_back(grad_after_low, out_mat, kept, tables, extra)
        down_back, in_back, sin_back = after((down_back, in_back, sin_back), grad_made)
        layer_out = after_attn + layer_out.astype(F32)
        small_grads = jnp.concatenate([grad_router_t, grad_gain_second], axis=0).T
        small_grads = jnp.pad(small_grads, ((0, 0), (3 * span, extra - experts - 1)))
        grad_qkv = (dot(normed_low.T, grad_made) + small_grads).astype(LOW)
        grad_first = dot(grad_made, attn_mat[:, : 3 * span + extra].T).astype(LOW).reshape(blocks, rows, width)
        grad_first = total(line_t.give([grad_first[i] for i in range(blocks)]))
        local_normed = first_normed[:rows]
        grad_inputs = grad_after + norm_back(
            grad_first, local_normed, first_scale[:rows], gain_first
        )

        grad_edown = side_by_side(*home(down_back)).astype(F32)
        kept, came = home(in_back)
        grad_egate = jnp.where(first, kept, came).astype(F32)
        grad_eup = jnp.where(first, came, kept).astype(F32)
        grad_outmat = lax.psum_scatter(grad_outmat, (Z, K), scatter_dimension=0, tiled=True)
        back = [(there, here) for here, there in move]
        grad_outmat = lax.ppermute(grad_outmat, (Z, K, C, D), back).astype(F32)
        grad_qkv = lax.psum_scatter(grad_qkv, (Z, K), scatter_dimension=0, tiled=True)
        grad_qkv = line_t.trade(grad_qkv.reshape(blocks, part, 3 * span + extra))
        sdown_back = line_t.trade(sdown_sums)
        grad_sin = total([sin_back[i] for i in range(blocks)]).astype(LOW)
        grad_sin = settle(line_z.give_from(grad_sin), col)
        grad_sin = grad_sin.transpose(1, 0, 2).astype(F32)
        grad_sgate = grad_sin[:, :, :hidden].reshape(part, -1)
        grad_sup = grad_sin[:, :, hidden:].reshape(part, -1)

        grad_sdown = total([sdown_back[i, 0] for i in range(blocks)])
        grad_qkv = grad_qkv.astype(F32)
        small_grads = jnp.sum(grad_qkv[:, :, 3 * span :], axis=0)
        grad_qkv = grad_qkv[:, :, : 3 * span].reshape(blocks, part, 3, span)
        grad_qkv = grad_qkv.transpose(2, 1, 0, 3).reshape(3, part, width)

        grad_gain_first = sum(
            jnp.sum(grad_qkv[i] * w.astype(F32), axis=1)
            for i, w in enumerate((w_query, w_key, w_value))
        ) / gain_attn.astype(F32)

        return (
            layer_out[None],
            grad_inputs[None],
            grad_gain_first,
            grad_qkv[0],
            grad_qkv[1],
            grad_qkv[2],
            grad_outmat,
            small_grads[:, experts],
            small_grads[:, :experts],
            grad_sgate,
            grad_sup,
            grad_sdown,
            grad_egate,
            grad_eup,
            grad_edown,
        )

    return body


def solution(mesh):
    owners, blocks, halves = mesh.devices.shape
    mesh = Mesh(mesh.devices.reshape(owners // 2, 2, blocks, halves), (Z, K, C, D))
    every = P((Z, K, C, D))
    tokens = P((Z, K), (C, D))
    return jax.shard_map(
        make_body(mesh),
        mesh=mesh,
        in_specs=(tokens, P((Z, K)), tokens) + (every,) * 10 + (tokens,) * 4,
        out_specs=(tokens, tokens) + (every,) * 10 + (tokens,) * 3,
        check_vma=False,
    )
```

```python
import math

import jax
import jax.numpy as jnp
from jax import lax
from jax.experimental import pallas as pl
from jax.experimental.pallas import tpu as pltpu
from jax.sharding import Mesh
from jax.sharding import PartitionSpec as P

HD = 128
TOP = 6
EPS = 1e-06
MASKED = -1e30
Z, K, C, D = "z", "core", "context", "dp"
F32 = jnp.float32
LOW = jnp.bfloat16


class Line:
    def __init__(self, mesh, *names):
        self.names = names
        self.size = math.prod(mesh.shape[name] for name in names)

    def at(self):
        return lax.axis_index(self.names)

    def swap(self, value, delta):
        return lax.ppermute(value, self.names, [(i, i ^ delta) for i in range(self.size)])

    def share(self, value):
        return [value] + [self.swap(value, delta) for delta in range(1, self.size)]

    def give(self, pieces):
        return [pieces[0]] + [self.swap(pieces[delta], delta) for delta in range(1, self.size)]

    def give_from(self, stack, dim=0):
        here = self.at()
        return self.give([pick(stack, here ^ delta, dim) for delta in range(self.size)])

    def trade(self, blocks):
        return lax.all_to_all(blocks, self.names, split_axis=0, concat_axis=0, tiled=True)


def pick(stack, index, dim=0):
    return lax.dynamic_index_in_dim(stack, index, dim, keepdims=False)


def settle(pieces, index, dim=0):
    shape = list(pieces[0].shape)
    shape.insert(dim, len(pieces))
    out = jnp.zeros(shape, pieces[0].dtype)
    for delta, piece in enumerate(pieces):
        out = lax.dynamic_update_index_in_dim(out, piece, index ^ delta, dim)
    return out


def in_order(first, mine, other):
    return jnp.where(first, mine, other), jnp.where(first, other, mine)


def after(value, *events):
    return lax.optimization_barrier((value, *events))[0]


def dot(left, right):
    return jnp.dot(left, right, preferred_element_type=F32)


def total(pieces):
    out = pieces[0].astype(F32)
    for piece in pieces[1:]:
        out = out + piece.astype(F32)
    return out


def norm_back(grad_normed, normed, scale, gain):
    scaled = grad_normed * gain
    return scale * (scaled - normed * jnp.mean(scaled * normed, axis=1, keepdims=True))


def swish_slope(values, sigma):
    return sigma * (1.0 + values * (1.0 - sigma))


def whole_spec(array):
    return pl.BlockSpec(array.shape, lambda j: (0,) * array.ndim)


def attention_probs(query, key, places, docs, places_row, docs_row):
    across = (((1,), (1,)), ((), ()))
    scores = lax.dot_general(query, key, across, preferred_element_type=F32) * HD ** (-0.5)
    allowed = (places >= places_row) & (docs == docs_row)
    scores = jnp.where(allowed, scores, MASKED)
    exponent = jnp.exp(scores - jnp.max(scores, axis=1, keepdims=True))
    return exponent / jnp.sum(exponent, axis=1, keepdims=True)


def attention_kernel(
    normed, w_q, w_k, w_v, w_o, cosine, sine, places, docs, places_row, docs_row,
    query, key, value, mixed, out, sums,
):
    step = pl.program_id(0)
    weights = jnp.concatenate([w_q[...], w_k[...], w_v[...]], axis=1)
    made = jnp.dot(normed[...], weights, preferred_element_type=F32)

    def rotated(values):
        swapped = pltpu.roll(values, HD // 2, axis=1)
        return (values * cosine[...] + swapped * sine[...]).astype(LOW)

    query[...] = rotated(made[:, :HD])
    key[...] = rotated(made[:, HD : 2 * HD])
    value[...] = made[:, 2 * HD :].astype(LOW)
    probs = attention_probs(
        query[...], key[...], places[...], docs[...], places_row[...], docs_row[...]
    )
    low = jnp.dot(probs.astype(LOW), value[...], preferred_element_type=F32).astype(LOW)
    mixed[...] = low
    part = jnp.dot(low, w_o[...], preferred_element_type=F32)

    @pl.when(step == 0)
    def _():
        sums[...] = part

    @pl.when(step > 0)
    def _():
        sums[...] += part

    @pl.when(step == pl.num_programs(0) - 1)
    def _():
        out[...] = sums[...].astype(LOW)


def attention_forward(normed, mats, out_mat, tables):
    length, width = normed.shape
    span = out_mat.shape[0]
    heads = span // HD
    head = lambda rows, first: pl.BlockSpec((rows, HD), lambda j: (0, first + j))
    shapes = [jax.ShapeDtypeStruct((length, span), LOW)] * 4
    shapes.append(jax.ShapeDtypeStruct((length, width), LOW))
    return pl.pallas_call(
        attention_kernel,
        grid=(heads,),
        in_specs=[
            whole_spec(normed),
            head(width, 0),
            head(width, heads),
            head(width, 2 * heads),
            pl.BlockSpec((HD, width), lambda j: (j, 0)),
        ]
        + [whole_spec(table) for table in tables],
        out_specs=[head(length, 0)] * 4 + [whole_spec(shapes[4])],
        out_shape=shapes,
        scratch_shapes=[pltpu.VMEM((length, width), F32)],
        compiler_params=pltpu.CompilerParams(vmem_limit_bytes=48 * 2**20),
        cost_estimate=pl.CostEstimate(
            flops=2 * length * span * (4 * width + 2 * length),
            bytes_accessed=2 * (2 * length * width + 4 * width * span + 4 * length * span),
            transcendentals=heads * length * length,
        ),
    )(normed, mats, mats, mats, out_mat, *tables)


def attention_back_kernel(
    grad_out, w_o, query, key, value, mixed, cosine, sine, places, docs, places_row, docs_row,
    grads, grad_w,
):
    step = pl.program_id(0)
    heads = (grads.shape[1] - 1) // (3 * HD)
    across = (((1,), (1,)), ((), ()))
    down = (((0,), (0,)), ((), ()))
    given = grad_out[...]
    grad_w[...] = lax.dot_general(mixed[...], given, down, preferred_element_type=F32).astype(LOW)
    low = lax.dot_general(given, w_o[...], across, preferred_element_type=F32).astype(LOW)
    probs = attention_probs(
        query[...], key[...], places[...], docs[...], places_row[...], docs_row[...]
    )
    grad_p = lax.dot_general(low, value[...], across, preferred_element_type=F32)
    grad_v = lax.dot_general(probs.astype(LOW), low, down, preferred_element_type=F32)
    grad_s = probs * (grad_p - jnp.sum(grad_p * probs, axis=1, keepdims=True))
    grad_s = grad_s.astype(LOW)
    scale = HD ** (-0.5)
    grad_q = jnp.dot(grad_s, key[...], preferred_element_type=F32) * scale
    grad_k = lax.dot_general(grad_s, query[...], down, preferred_element_type=F32) * scale

    def unrotated(values):
        swapped = pltpu.roll(values, HD // 2, axis=1)
        return (values * cosine[...] - swapped * sine[...]).astype(LOW)

    def column(first):
        return pl.ds(pl.multiple_of((first * heads + step) * HD, HD), HD)

    grads[:, column(0)] = unrotated(grad_q)
    grads[:, column(1)] = unrotated(grad_k)
    grads[:, column(2)] = grad_v.astype(LOW)

    @pl.when(step == 0)
    def _():
        rest = grads.shape[1] - 3 * HD * heads
        grads[:, 3 * HD * heads :] = jnp.zeros((grads.shape[0], rest), LOW)


def attention_back(grad_out, out_mat, kept, tables, extra):
    length, width = grad_out.shape
    span = out_mat.shape[0]
    heads = span // HD
    head = pl.BlockSpec((length, HD), lambda j: (0, j))
    row = pl.BlockSpec((HD, width), lambda j: (j, 0))
    shapes = [
        jax.ShapeDtypeStruct((length, 3 * span + extra), LOW),
        jax.ShapeDtypeStruct((span, width), LOW),
    ]

    return pl.pallas_call(
        attention_back_kernel,
        grid=(heads,),
        in_specs=[whole_spec(grad_out), row] + [head] * 4 + [whole_spec(t) for t in tables],
        out_specs=[whole_spec(shapes[0]), row],
        out_shape=shapes,
        compiler_params=pltpu.CompilerParams(vmem_limit_bytes=48 * 2**20),
        cost_estimate=pl.CostEstimate(
            flops=2 * length * span * (2 * width + 5 * length),
            bytes_accessed=2 * (length * width + 2 * width * span + 7 * length * span),
            transcendentals=heads * length * length,
        ),
    )(grad_out, out_mat, *kept, *tables)


def expert_kernel(flag, slots, mine, other, raw, gate, hidden, grads, dgate):
    step = pl.program_id(0)
    tile = mine.shape[1]
    wide = grads.shape[1] // 2
    is_first = flag[0] == 1
    weights = jnp.concatenate([mine[...], other[...]], axis=1)
    count = slots.shape[0]
    chunk = min(count, 256)
    left_at = pl.multiple_of(step * tile, tile)
    right_at = pl.multiple_of(wide + step * tile, tile)
    for at in range(0, count, chunk):
        here = slice(at, at + chunk)
        made = jnp.dot(slots[here, :], weights, preferred_element_type=F32)
        left, right = made[:, :tile], made[:, tile:]
        a = jnp.where(is_first, left, right)
        b = jnp.where(is_first, right, left)
        sigma = jax.nn.sigmoid(a)
        silu = a * sigma
        low = (silu * b).astype(LOW)
        hidden[here, :] = low
        du = raw[here, :]
        part = jnp.sum(low.astype(F32) * du, axis=1, keepdims=True)
        du = du * gate[here, :]
        da = du * b * (sigma * (1.0 + a * (1.0 - sigma)))
        db = du * silu
        grads[here, pl.ds(left_at, tile)] = jnp.where(is_first, da, db).astype(LOW)
        grads[here, pl.ds(right_at, tile)] = jnp.where(is_first, db, da).astype(LOW)
        dgate[here, :] = part + jnp.where(step == 0, 0.0, dgate[here, :])


def expert_forward(flag, slots, mine, other, raw, gate):
    count, width = slots.shape
    wide = mine.shape[1]
    tile = 128
    column = lambda rows: pl.BlockSpec((rows, tile), lambda j: (0, j))
    shapes = (
        jax.ShapeDtypeStruct((count, wide), LOW),
        jax.ShapeDtypeStruct((count, 2 * wide), LOW),
        jax.ShapeDtypeStruct((count, 1), F32),
    )
    return pl.pallas_call(
        expert_kernel,
        grid=(wide // tile,),
        in_specs=[
            pl.BlockSpec(memory_space=pltpu.SMEM),
            whole_spec(slots),
            column(width),
            column(width),
            column(count),
            whole_spec(gate),
        ],
        out_specs=(column(count), whole_spec(shapes[1]), whole_spec(shapes[2])),
        out_shape=shapes,
        compiler_params=pltpu.CompilerParams(vmem_limit_bytes=48 * 2**20),
        cost_estimate=pl.CostEstimate(
            flops=4 * count * width * wide,
            bytes_accessed=2 * (count * width + 2 * width * wide + 5 * count * wide),
            transcendentals=count * wide,
        ),
    )(flag, slots, mine, other, raw, gate)


def back_kernel(flag, grads, mine, other, dgate, out):
    step = pl.program_id(0)
    tile = mine.shape[0]
    wide = grads.shape[1] // 2
    width = out.shape[1] - 128
    across = (((1,), (1,)), ((), ()))
    made = lax.dot_general(grads[:, :wide], mine[...], across, preferred_element_type=F32)
    made += lax.dot_general(grads[:, wide:], other[...], across, preferred_element_type=F32)
    out[:, pl.ds(pl.multiple_of(step * tile, tile), tile)] = made.astype(LOW)

    @pl.when(step == 0)
    def _():
        lanes = lax.broadcasted_iota(jnp.int32, (out.shape[0], 128), 1)
        high = dgate[...].astype(LOW).astype(F32)
        rest = dgate[...] - high
        cols = jnp.where(lanes == flag[1], high, jnp.where(lanes == flag[1] + 64, rest, 0.0))
        out[:, width:] = cols.astype(LOW)


def expert_back(flag, grads, mine, other, dgate):
    count = grads.shape[0]
    width, wide = mine.shape
    tile = 256
    shape = jax.ShapeDtypeStruct((count, width + 128), LOW)
    row = pl.BlockSpec((tile, wide), lambda j: (j, 0))
    return pl.pallas_call(
        back_kernel,
        grid=(width // tile,),
        in_specs=[
            pl.BlockSpec(memory_space=pltpu.SMEM),
            whole_spec(grads),
            row,
            row,
            whole_spec(dgate),
        ],
        out_specs=whole_spec(shape),
        out_shape=shape,
        compiler_params=pltpu.CompilerParams(vmem_limit_bytes=48 * 2**20),
        cost_estimate=pl.CostEstimate(
            flops=4 * count * width * wide,
            bytes_accessed=2 * (2 * count * wide + 2 * width * wide + count * width),
            transcendentals=0,
        ),
    )(flag, grads, mine, other, dgate)


def make_body(mesh):
    line_z, line_k, line_t = Line(mesh, Z), Line(mesh, K), Line(mesh, C, D)
    columns, cores, blocks = line_z.size, line_k.size, line_t.size
    owners = columns * cores

    def body(
        tokens_in,
        doc_ids,
        routes,
        gain_attn,
        w_query,
        w_key,
        w_value,
        w_out,
        gain_moe,
        w_router,
        shared_gate,
        shared_up,
        shared_down,
        expert_gate,
        expert_up,
        expert_down,
        cotangent,
    ):
        col, core, blk = line_z.at(), line_k.at(), line_t.at()
        x_low, dy_low = tokens_in[0], cotangent[0]
        rows, width = x_low.shape
        length = doc_ids.shape[1]
        part = w_query.shape[0]
        span = width // blocks
        heads = span // HD
        experts = w_router.shape[1]
        group = experts // columns
        line_s = line_t if blocks == group else Line(mesh, C)
        rest = () if blocks == group else (D,)
        spot = line_s.at()

        first = core == 0
        half = width // 2

        def column_halves(value):
            return in_order(first, value[..., :half], value[..., half:])

        def side_by_side(mine, other):
            return jnp.concatenate(in_order(first, mine, other), axis=-1)

        def both_cores(mine, other):
            return jnp.concatenate(in_order(first, mine, line_k.swap(other, 1)), axis=0)

        def all_rows(whole):
            if rest:
                whole = lax.all_gather(whole, rest, axis=1, tiled=True)
            return whole.reshape(-1, whole.shape[-1])

        down_part = both_cores(*column_halves(expert_down))
        in_part = both_cores(*in_order(first, expert_gate, expert_up))

        small = jnp.concatenate([w_router, gain_attn[:, None], gain_moe[:, None]], axis=1)
        small = jnp.pad(small, ((0, 0), (0, -small.shape[1] % 128)))
        extra = small.shape[1]
        mixed_in = jnp.concatenate(
            [w.reshape(part, blocks, span) for w in (w_query, w_key, w_value)]
            + [jnp.broadcast_to(small[:, None], (part, blocks, extra))],
            axis=2,
        ).transpose(1, 0, 2)
        move = [(i, (i % owners) * blocks + i // owners) for i in range(owners * blocks)]
        out_part = lax.ppermute(w_out, (Z, K, C, D), move)
        out_part = out_part.reshape(part, blocks, span).transpose(1, 0, 2)
        attn_part = settle(line_t.give_from(mixed_in), blk)
        attn_part = jnp.concatenate([attn_part, out_part], axis=2).reshape(blocks * part, -1)
        attn_mat = lax.all_gather(attn_part, (Z, K), axis=0, tiled=True)
        dy_col = lax.all_gather(after(dy_low, attn_mat), Z, axis=0, tiled=True)

        x_got = line_t.share(x_low)
        down_got = line_s.trade(down_part)
        routes_got = line_z.share(routes[0])
        down_got, in_part, x_got, routes_got = lax.optimization_barrier(
            (down_got, in_part, x_got, routes_got)
        )
        in_got = line_s.trade(in_part)
        routes_col = settle(routes_got, col)
        x_all = jnp.concatenate(x_got, axis=0).astype(F32)
        small = attn_mat[:, 3 * span : 3 * span + extra].T
        router_t = small[:experts]
        gain_first = small[experts].astype(F32)[None]
        gain_second = small[experts + 1].astype(F32)[None]
        out_mat = attn_mat[:, 3 * span + extra :].reshape(owners, blocks, part, span)
        out_mat = out_mat.transpose(0, 2, 1, 3).reshape(owners * part, width)

        doc_row = doc_ids[0]
        order = blk ^ jnp.arange(blocks, dtype=jnp.int32)
        doc_starts = jnp.sum((doc_row[None, :] < doc_row[:, None]).astype(jnp.int32), axis=1)
        offsets = jnp.arange(length, dtype=jnp.int32) - doc_starts

        def reorder(row):
            grid = row.reshape(blocks, rows)
            return jnp.concatenate([pick(grid, order[i]) for i in range(blocks)])

        doc_here, off_here = reorder(doc_row), reorder(offsets)
        place = reorder(jnp.arange(length, dtype=jnp.int32))
        frequency = jnp.exp(
            jnp.arange(HD // 2, dtype=F32) * (-math.log(10000.0) / (HD // 2))
        )
        angles = off_here.astype(F32)[:, None] * frequency[None, :]
        cosine, sine = jnp.cos(angles), jnp.sin(angles)
        tables = (
            jnp.concatenate([cosine, cosine], axis=1),
            jnp.concatenate([-sine, sine], axis=1),
            place[:, None],
            doc_here[:, None],
            place[None, :],
            doc_here[None, :],
        )

        first_scale = lax.rsqrt(jnp.mean(x_all * x_all, axis=1, keepdims=True) + EPS)
        first_normed = x_all * first_scale
        normed_low = (first_normed * gain_first).astype(LOW)
        *kept, attn_out = attention_forward(normed_low, attn_mat, out_mat, tables)
        attn_out = attn_out.reshape(blocks, rows, width)

        hidden = shared_gate.shape[1] // columns
        shared_in = jnp.concatenate(
            [w.reshape(part, columns, hidden).transpose(1, 0, 2) for w in (shared_gate, shared_up)],
            axis=2,
        )

        in_got = after(in_got, attn_out)
        inputs = after(x_low, in_got).astype(F32)
        after_attn = inputs + total(line_t.give([attn_out[i] for i in range(blocks)]))

        second_scale = lax.rsqrt(jnp.mean(after_attn * after_attn, axis=1, keepdims=True) + EPS)
        second_normed = after_attn * second_scale
        second_low = (second_normed * gain_second).astype(LOW)
        second_col = lax.all_gather(second_low, Z, axis=0, tiled=True)
        mat_down = all_rows(after(down_got, second_low))
        mat_down = side_by_side(mat_down, line_k.swap(mat_down, 1))
        mat_mine = all_rows(after(in_got, second_low))
        mat_other = line_k.swap(mat_mine, 1)
        shared_in = settle(line_z.give_from(after(shared_in, second_col)), col)

        def router(values):
            return jax.nn.softmax(dot(values, router_t.T), axis=1)

        router_probs = router(second_low)

        capacity = min(rows, rows * TOP * 4 // (3 * experts))
        slots = columns * capacity
        wanted = col * group + jnp.arange(group, dtype=jnp.int32)
        hits = jnp.any(routes_col[None] == wanted[:, None, None, None], axis=3)
        ranks = jnp.cumsum(hits.astype(jnp.int32), axis=2) - 1
        ranks = jnp.where(hits, ranks, -1)
        chosen = ranks[:, :, None, :] == jnp.arange(capacity, dtype=jnp.int32)[:, None]
        same = jnp.eye(columns, dtype=jnp.bool_)[None, :, None, :, None]
        spread = (
            (chosen[:, :, :, None, :] & same).reshape(group * slots, columns * rows).astype(LOW)
        )

        def dispatch(values):
            sent = dot(spread, values).astype(LOW).reshape(group, slots, width)
            return line_s.trade(sent).reshape(group * slots, width)

        def collect(values):
            return line_s.trade(values.reshape(group, slots, -1)).reshape(group * slots, -1)

        dy_slots = dispatch(dy_col)
        du_raw = dot(dy_slots, mat_down.T)
        second_slots = after(dispatch(after(second_col, dy_slots)), du_raw, mat_other)
        expert = col * group + spot
        gate = lax.dynamic_slice_in_dim(router(second_slots), expert, 1, axis=1)
        flag = jnp.stack([first.astype(jnp.int32), expert])
        hidden_low, grad_in, dgate = expert_forward(
            flag, second_slots, mat_mine, mat_other, du_raw, gate
        )
        wide = hidden_low.shape[1]

        cuts = -(-width // (2 * hidden))
        down_cuts = jnp.pad(shared_down, ((0, 0), (0, cuts * 2 * hidden - width)))
        shared_part = jnp.concatenate(
            [shared_in.reshape(columns * part, 2 * hidden)] + jnp.split(down_cuts, cuts, axis=1)
        )
        shared_all = lax.all_gather(after(shared_part, second_slots), (K, C, D), axis=0)
        grad_slots = expert_back(flag, grad_in, mat_mine, mat_other, dgate)

        shared_all = after(shared_all, grad_slots)
        mat_sin = shared_all[:, : columns * part].reshape(-1, columns, part, 2 * hidden)
        mat_sin = mat_sin.transpose(1, 0, 2, 3).reshape(width, 2 * hidden)
        mat_sdown = jnp.concatenate(jnp.split(shared_all[:, columns * part :], cuts, axis=1), axis=2)
        mat_sdown = mat_sdown[:, :, :width].reshape(hidden, width)
        second_late, dy_late = after((second_col, dy_col), grad_slots)
        shared_pre = dot(second_late, mat_sin)
        shared_a, shared_b = shared_pre[:, :hidden], shared_pre[:, hidden:]
        shared_sigma = jax.nn.sigmoid(shared_a)
        shared_low = (shared_a * shared_sigma * shared_b).astype(LOW)
        dsu = dot(dy_late, mat_sdown.T)
        dsa = (dsu * shared_b * swish_slope(shared_a, shared_sigma)).astype(LOW)
        dsb = (dsu * shared_a * shared_sigma).astype(LOW)
        dsab = jnp.concatenate([dsa, dsb], axis=1)

        routed = (dot(after(hidden_low, dsab), mat_down) * gate).astype(LOW)
        def both_parts(mine, other):
            return [mine, line_k.swap(other, 1)]

        def low_total(pieces):
            return total(pieces).astype(LOW)

        def shared_home(grad):
            lead, count, wide = grad.shape
            grad = grad.reshape(lead, cores, count // cores, wide)
            return both_parts(*in_order(first, grad[:, 0], grad[:, 1]))

        def by_owner(mine):
            lead, count, wide = mine.shape
            return mine.reshape(lead, blocks, count // blocks, wide).transpose(1, 0, 2, 3)

        slots_back = collect(grad_slots)
        grad_routed = dot(spread.T, after(slots_back, routed))
        grad_second = jnp.concatenate(
            [dot(dsab, mat_sin.T) + grad_routed[:, :width], grad_routed[:, width:]], axis=1
        )
        second_sent = grad_second.astype(LOW)
        grad_second = lax.psum_scatter(second_sent, Z, scatter_dimension=0, tiled=True).astype(F32)


        def send_home(mine):
            mine = mine.reshape(line_s.size, -1, mine.shape[-1])
            if rest:
                mine = lax.psum_scatter(mine, rest, scatter_dimension=1, tiled=True)
            return mine

        def home(got):
            got = got.reshape(cores, -1, *got.shape[1:])
            kept, other = in_order(first, got[0], got[1])
            return kept, line_k.swap(other, 1)

        weighted = (hidden_low.astype(F32) * gate).astype(LOW)
        slots_late = after(second_slots, grad_slots)
        grad_w = dot(slots_late.T, grad_in).astype(LOW)

        routed_back = collect(after(routed, grad_routed))
        grad_down = dot(weighted.T, dy_slots).astype(LOW)
        grad_second, grad_w = lax.optimization_barrier((grad_second, grad_w))
        routed_back, grad_down = lax.optimization_barrier((routed_back, grad_down))
        down_sums = low_total(both_parts(*column_halves(grad_down)))

        dprobs = grad_second[:, width : width + experts]
        dprobs = dprobs + grad_second[:, width + 64 : width + 64 + experts]
        dlogits = (
            router_probs * (dprobs - jnp.sum(dprobs * router_probs, axis=1, keepdims=True))
        ).astype(LOW)
        grad_router_t = dot(dlogits.T, second_low)
        grad_second = grad_second[:, :width] + dot(dlogits, router_t)

        grad_gain_second = jnp.sum(grad_second * second_normed, axis=0, keepdims=True)
        dy = dy_low.astype(F32)
        grad_after = dy + norm_back(grad_second, second_normed, second_scale, gain_second)
        grad_after_low, routed_back = lax.optimization_barrier(
            (grad_after.astype(LOW), routed_back)
        )
        grad_after_low = jnp.concatenate(line_t.share(grad_after_low), axis=0)
        grad_made, grad_outmat = attention_back(grad_after_low, out_mat, kept, tables, extra)
        small_grads = jnp.concatenate([grad_router_t, grad_gain_second], axis=0).T
        small_grads = jnp.pad(small_grads, ((0, 0), (3 * span, extra - experts - 1)))
        grad_qkv = (dot(normed_low.T, grad_made) + small_grads).astype(LOW)
        grad_first = dot(grad_made, attn_mat[:, : 3 * span + extra].T).astype(LOW).reshape(blocks, rows, width)
        grad_w_other = line_k.swap(grad_w[:, wide:], 1)
        grad_qkv, grad_first, dsab, grad_w, grad_w_other = lax.optimization_barrier(
            (grad_qkv, grad_first, dsab, grad_w, grad_w_other)
        )
        in_back = line_s.trade(send_home(low_total([grad_w[:, :wide], grad_w_other])))
        grad_first = total(line_t.give([grad_first[i] for i in range(blocks)]))
        grad_first, dsab, routed_back = lax.optimization_barrier((grad_first, dsab, routed_back))
        layer_sent = (dot(shared_low, mat_sdown) + dot(spread.T, routed_back)).astype(LOW)
        layer_out = lax.psum_scatter(layer_sent, Z, scatter_dimension=0, tiled=True)
        layer_out = after_attn + layer_out.astype(F32)
        grad_sin = dot(second_late.T, dsab).astype(LOW)
        grad_sdown = dot(shared_low.T, dy_late).astype(LOW)
        sin_sums = shared_home(grad_sin.reshape(columns, cores * blocks * part, 2 * hidden))
        sin_sums = by_owner(low_total(sin_sums))
        sdown_sums = by_owner(low_total(shared_home(grad_sdown[None])))
        local_normed = first_normed[:rows]
        grad_inputs = grad_after + norm_back(
            grad_first, local_normed, first_scale[:rows], gain_first
        )

        grad_outmat = lax.psum_scatter(grad_outmat, (Z, K), scatter_dimension=0, tiled=True)
        back = [(there, here) for here, there in move]
        grad_outmat = lax.ppermute(grad_outmat, (Z, K, C, D), back).astype(F32)
        grad_qkv = lax.psum_scatter(grad_qkv, (Z, K), scatter_dimension=0, tiled=True)
        grad_qkv, in_back = lax.optimization_barrier((grad_qkv, in_back))
        grad_qkv = line_t.trade(grad_qkv.reshape(blocks, part, 3 * span + extra))
        kept, came = home(in_back)
        grad_egate = jnp.where(first, kept, came).astype(F32)
        grad_eup = jnp.where(first, came, kept).astype(F32)
        grad_qkv, down_sums, sin_sums, sdown_sums = lax.optimization_barrier(
            (grad_qkv, down_sums, sin_sums, sdown_sums)
        )
        sin_back = line_t.trade(sin_sums)
        sin_back, down_sums, sdown_sums = lax.optimization_barrier((sin_back, down_sums, sdown_sums))
        sdown_back = line_t.trade(sdown_sums)
        down_back = line_s.trade(send_home(down_sums))
        grad_edown = side_by_side(*home(down_back)).astype(F32)
        grad_sin = total([sin_back[i] for i in range(blocks)]).astype(LOW)
        grad_sin = settle(line_z.give_from(grad_sin), col)
        grad_sin = grad_sin.transpose(1, 0, 2).astype(F32)
        grad_sgate = grad_sin[:, :, :hidden].reshape(part, -1)
        grad_sup = grad_sin[:, :, hidden:].reshape(part, -1)

        grad_sdown = total([sdown_back[i, 0] for i in range(blocks)])
        grad_qkv = grad_qkv.astype(F32)
        small_grads = jnp.sum(grad_qkv[:, :, 3 * span :], axis=0)
        grad_qkv = grad_qkv[:, :, : 3 * span].reshape(blocks, part, 3, span)
        grad_qkv = grad_qkv.transpose(2, 1, 0, 3).reshape(3, part, width)

        grad_gain_first = sum(
            jnp.sum(grad_qkv[i] * w.astype(F32), axis=1)
            for i, w in enumerate((w_query, w_key, w_value))
        ) / gain_attn.astype(F32)

        return (
            layer_out[None],
            grad_inputs[None],
            grad_gain_first,
            grad_qkv[0],
            grad_qkv[1],
            grad_qkv[2],
            grad_outmat,
            small_grads[:, experts],
            small_grads[:, :experts],
            grad_sgate,
            grad_sup,
            grad_sdown,
            grad_egate,
            grad_eup,
            grad_edown,
        )

    return body


def solution(mesh):
    owners, blocks, halves = mesh.devices.shape
    mesh = Mesh(mesh.devices.reshape(owners // 2, 2, blocks, halves), (Z, K, C, D))
    every = P((Z, K, C, D))
    tokens = P((Z, K), (C, D))
    return jax.shard_map(
        make_body(mesh),
        mesh=mesh,
        in_specs=(tokens, P((Z, K)), tokens) + (every,) * 10 + (tokens,) * 4,
        out_specs=(tokens, tokens) + (every,) * 10 + (tokens,) * 3,
        check_vma=False,
    )
```
